32 devices in a mesh: px: 4 (over x, core), py: 8 (over z, y).
Axes of the slice: x: 2, y: 2, z: 4, core: 2. Of those that a mesh axis runs over, the one named last changes fastest.
Arguments:
- theta: float32 [58, 64, 2048], P(None, 'px', 'py'), may hold values from 0.5 to 1.5
- vapor: float32 [58, 64, 2048], P(None, 'px', 'py'), may hold values from 0.1 to 1
- cloud: float32 [58, 64, 2048], P(None, 'px', 'py'), may hold values from 0 to 0.4
- divergence: float32 [58, 64, 2048], P(None, 'px', 'py'), may hold values from -6 to 6
- edge_weight: float32 [3, 64, 2048], P(None, 'px', 'py'), may hold values from 0.5 to 2
- inv_area: float32 [64, 2048], P('px', 'py'), may hold values from 0.7 to 1.4
- damping: float32 [3, 58], replicated, may hold values from 0.0005 to 0.004
- exner: float32 [58], replicated, may hold values from 0.6 to 1
- sat_scale: float32 [58], replicated, may hold values from 0.1 to 0.6
- layer_mass: float32 [58], replicated, may hold values from 0.02 to 0.1
- span_of: int32 [64, 2048], P('px', 'py'), may hold values from 0 to 32767, as said below
Outputs:
- theta_next: float32 [58, 64, 2048], P(None, 'px', 'py')
- vapor_next: float32 [58, 64, 2048], P(None, 'px', 'py')
- cloud_next: float32 [58, 64, 2048], P(None, 'px', 'py')
- divergence_next: float32 [58, 64, 2048], P(None, 'px', 'py')
- precip_spans: float32 [4, 32768], P('px', 'py')
The draws below stay inside these ranges and needn't reach their ends.
Inputs may be any that keep to these rules, and one draw needn't show every extreme that they name: `span_of`: position p of px index a belongs to device p // 4096 of the py row of a. Within the 16 rows of one px index the entries are a permutation. The columns of one device take exactly 384 positions of every device of its row and 1024 more positions of one other device of that row, so each device receives exactly 4096 positions.
All inputs are finite; a program needn't handle non-finite values.
Results may differ from the reference program's by a relative error of at most 0.00002.
Values sent between devices are 32-bit elements; how exact they have to be, the bound alone decides.
A program may use at most 128 MiB of HBM per device.

```python
import math
import jax
import jax.numpy as jnp

L = 58
CX = 16
CY = 256
NSAT = 2
NX = 64
NY = 2048
N_PX = 4
N_PY = 8


def row_positions(row_key):
    peers = N_PY
    column_total = CX * CY
    quarter = column_total // 4
    group_size = 3 * column_total // (4 * peers)
    partner_shift = jax.random.randint(jax.random.fold_in(row_key, 1), (), 1, peers)
    source_orders = jax.vmap(lambda sub_key: jax.random.permutation(sub_key, column_total))(jax.random.split(jax.random.fold_in(row_key, 2), peers))
    target_orders = jax.vmap(lambda sub_key: jax.random.permutation(sub_key, column_total))(jax.random.split(jax.random.fold_in(row_key, 3), peers))
    places = jnp.arange(column_total, dtype=jnp.int32)[None, :]
    sources = jnp.arange(peers, dtype=jnp.int32)[:, None]
    in_group = places >= quarter
    target = jnp.where(in_group, (places - quarter) // group_size, (sources + partner_shift) % peers)
    arrival = jnp.where(in_group, sources * group_size + (places - quarter) % group_size, peers * group_size + places)
    placed = target * column_total + jnp.take(target_orders.reshape(-1), target * column_total + arrival)
    result = jnp.zeros((peers, column_total), jnp.int32).at[sources, source_orders].set(placed.astype(jnp.int32))
    return result


def draw_span_of(key, part):
    row_keys = jax.random.split(jax.random.fold_in(key, 7), N_PX)
    blocks = jax.vmap(row_positions)(row_keys)
    blocks = blocks.reshape(N_PX, N_PY, CX, CY).transpose(0, 2, 1, 3)
    return blocks.reshape(NX, NY).astype(jnp.int32)


def block_levels(rng, dims, shards, low, high):
    def one(position, parts):
        draws = jax.random.uniform(jax.random.fold_in(jax.random.fold_in(rng, 6), position), (parts,), jnp.float32, low / len(shards), high / len(shards))
        return jnp.repeat(jnp.exp(draws), dims[position] // parts).reshape((-1,) + (1,) * (len(dims) - position - 1))

    loudness = one(*shards[0])
    for cut in shards[1:]:
        loudness = loudness * one(*cut)
    return loudness


def bell_draw(own_key, dims, width, limit, cuts=(), held_as=jnp.bfloat16):
    drawn = jax.random.normal(own_key, dims, jnp.float32) * width
    if len(cuts) > 0:
        drawn = block_levels(own_key, dims, cuts, -0.22, 0.18) * drawn
    return jnp.clip(drawn, min=-limit, max=limit).astype(held_as)


def setup_inputs(seed: int = 0) -> dict:
    seeds = jax.random.split(jax.random.key(seed), 12)
    theta = jnp.clip(0.5 + 1.0 * jax.random.uniform(seeds[0], (L, NX, NY), jnp.float32) ** block_levels(seeds[0], (L, NX, NY), ((1, 4), (2, 8)), -0.2, 0.2), 0.5, 1.5)
    vapor = jnp.clip(0.1 + 0.9 * jax.random.uniform(seeds[1], (L, NX, NY), jnp.float32) ** block_levels(seeds[1], (L, NX, NY), ((1, 4), (2, 8)), -0.2, 0.2), 0.1, 1.0)
    cloud = jnp.clip(0.4 * jax.random.uniform(seeds[2], (L, NX, NY), jnp.float32) ** block_levels(seeds[2], (L, NX, NY), ((1, 4), (2, 8)), -0.2, 0.2), 0.0, 0.4)
    divergence = bell_draw(seeds[3], (L, NX, NY), 1.0, 6.0, ((1, 4), (2, 8)), jnp.float32)
    edge_weight = jnp.clip(jnp.exp(math.log(2.0) - 1.3862944 * jax.random.uniform(seeds[4], (3, NX, NY), jnp.float32) ** block_levels(seeds[4], (3, NX, NY), ((1, 4), (2, 8)), -0.2, 0.2)), 0.5, 2.0)
    inv_area = jnp.clip(jnp.exp(math.log(1.4) - 0.6931472 * jax.random.uniform(seeds[5], (NX, NY), jnp.float32) ** block_levels(seeds[5], (NX, NY), ((0, 4), (1, 8)), -0.2, 0.2)), 0.7, 1.4)
    damping = jnp.clip(jnp.exp(jax.random.uniform(seeds[6], (3, L), jnp.float32, math.log(0.0005), math.log(0.004))), 0.0005, 0.004)
    exner = jnp.clip(jnp.exp(jax.random.uniform(seeds[7], (L,), jnp.float32, math.log(0.6), math.log(1.0))), 0.6, 1.0)
    sat_scale = jnp.clip(jnp.exp(jax.random.uniform(seeds[8], (L,), jnp.float32, math.log(0.1), math.log(0.6))), 0.1, 0.6)
    layer_mass = jnp.clip(jnp.exp(jax.random.uniform(seeds[9], (L,), jnp.float32, math.log(0.02), math.log(0.1))), 0.02, 0.1)
    span_of = draw_span_of(jax.random.fold_in(seeds[11], 71), 0)
    return {"theta": theta, "vapor": vapor, "cloud": cloud, "divergence": divergence, "edge_weight": edge_weight, "inv_area": inv_area, "damping": damping, "exner": exner, "sat_scale": sat_scale, "layer_mass": layer_mass, "span_of": span_of}


LATENT = 0.5
QCRIT = 0.2
AUTO_RATE = 0.5


def shifted(array_in, step_row, step_col):
    height = array_in.shape[-2]
    breadth = array_in.shape[-1]
    return array_in[..., 1 + step_row:height - 1 + step_row, 1 + step_col:breadth - 1 + step_col]


def laplace(values, weights, inverse):
    centre = shifted(values, 0, 0)
    summed = shifted(weights[0], 0, 0) * (shifted(values, 1, 0) - centre)
    summed = summed + shifted(weights[0], -1, 0) * (shifted(values, -1, 0) - centre)
    summed = summed + shifted(weights[1], 0, 0) * (shifted(values, 0, 1) - centre)
    summed = summed + shifted(weights[1], 0, -1) * (shifted(values, 0, -1) - centre)
    summed = summed + shifted(weights[2], 0, 0) * (shifted(values, -1, 1) - centre)
    summed = summed + shifted(weights[2], 1, -1) * (shifted(values, 1, -1) - centre)
    return shifted(inverse, 0, 0) * summed


def adjust(theta_dyn, vapor_dyn, cloud, exner, sat_scale, layer_mass):
    temper = theta_dyn * exner
    condensed = jnp.zeros_like(theta_dyn)
    for repeat in range(NSAT):
        warmed = temper + LATENT * condensed
        saturation = sat_scale * jnp.exp(warmed)
        excess = vapor_dyn - condensed - saturation
        slope = -1.0 - LATENT * saturation
        condensed = condensed - excess / slope
    condensed = jnp.maximum(condensed, -cloud)
    theta_next = theta_dyn + LATENT * condensed / exner
    vapor_next = vapor_dyn - condensed
    liquid = cloud + condensed
    rained = AUTO_RATE * jnp.maximum(liquid - QCRIT, 0.0)
    cloud_next = liquid - rained
    precip = jnp.sum(layer_mass * rained, axis=0)
    return theta_next, vapor_next, cloud_next, precip


def reference(theta, vapor, cloud, divergence, edge_weight, inv_area, damping, exner, sat_scale, layer_mass, span_of):
    fields = jnp.concatenate([theta, vapor, divergence], 0)
    geometry = jnp.concatenate([edge_weight, inv_area[None]], 0)
    padded = jnp.pad(fields, ((0, 0), (2, 2), (2, 2)), mode="wrap")
    geometry_pad = jnp.pad(geometry, ((0, 0), (2, 2), (2, 2)), mode="wrap")
    lap_once = laplace(padded, geometry_pad[:3], geometry_pad[3])
    inner_geo = geometry_pad[:, 1:-1, 1:-1]
    second = laplace(lap_once, inner_geo[:3], inner_geo[3])
    damped = fields - damping.reshape(3 * L)[:, None, None] * second
    theta_next, vapor_next, cloud_next, precip = adjust(
        damped[:L], damped[L:2 * L], cloud,
        exner[:, None, None], sat_scale[:, None, None], layer_mass[:, None, None])
    divergence_next = damped[2 * L:]
    rain_rows = precip.reshape(N_PX, CX * NY)
    place_rows = span_of.reshape(N_PX, CX * NY)

    def place_row(places, rainfall):
        return jnp.zeros((CX * NY,), jnp.float32).at[places].set(rainfall)

    precip_spans = jax.vmap(place_row)(place_rows, rain_rows)
    return theta_next, vapor_next, cloud_next, divergence_next, precip_spans
```

```python
import functools

import jax
import jax.numpy as jnp
from jax import lax
from jax.experimental import pallas as pl
from jax.experimental.pallas import tpu as pltpu
from jax.sharding import PartitionSpec as P

NSAT = 2
LATENT = 0.5
QCRIT = 0.2
AUTO_RATE = 0.5

MESH = pl.DeviceIdType.MESH
LANES = 128
SUB = 8
CORNERS = ((1, 1), (1, -1), (-1, 1), (-1, -1))


def kernel(
    dims,
    theta,
    vapor,
    divergence,
    cloud,
    edge_weight,
    inv_area,
    span_of,
    damping,
    exner,
    sat_scale,
    layer_mass,
    theta_out,
    vapor_out,
    cloud_out,
    divergence_out,
    precip_out,
    nat,
    out,
    grid,
    lap,
    coef,
    consts,
    weights,
    areas,
    spans,
    col_send,
    col_recv,
    corner_send,
    corner_recv,
    high,
    low,
    rain_send,
    rain_recv,
    in_sem,
    out_sem,
    send_sem,
    recv_sem,
    rain_send_sem,
    rain_recv_sem,
):
    n_px, n_py, levels, rows, cols = dims
    pad = consts.shape[1]
    halves = cols // LANES
    groups = 3 * pad // SUB
    wide = cols + LANES
    block = rows * cols // LANES
    px = lax.axis_index("px")
    py = lax.axis_index("py")
    used = levels * rows

    def device(dx, dy):
        return (lax.rem(px + dx + n_px, n_px), lax.rem(py + dy + n_py, n_py))

    loads = []
    for f, source in enumerate((theta, vapor, divergence, cloud)):
        for h in range(halves):
            loads.append(
                pltpu.make_async_copy(
                    source.at[:, pl.ds(h * LANES, LANES)],
                    nat.at[f, h, pl.ds(0, used), :],
                    in_sem.at[len(loads)],
                )
            )
    for source, target in ((edge_weight, weights), (inv_area, areas), (span_of, spans)):
        loads.append(pltpu.make_async_copy(source, target, in_sem.at[len(loads)]))
    for load in loads:
        load.start()

    barrier = pltpu.get_barrier_semaphore()
    greeted = [(1, 0), (-1, 0)] + list(CORNERS) + [(0, d) for d in range(1, n_py)]
    for dx, dy in greeted:
        pl.semaphore_signal(barrier, inc=1, device_id=device(dx, dy), device_id_type=MESH)

    def fill(level, carry):
        at = pl.ds(level, 1)
        for k in range(3):
            consts[k, at, :] = jnp.full((1, LANES), damping[k, level], jnp.float32)
        consts[3, at, :] = jnp.full((1, LANES), exner[level], jnp.float32)
        consts[4, at, :] = jnp.full((1, LANES), sat_scale[level], jnp.float32)
        consts[5, at, :] = jnp.full((1, LANES), layer_mass[level], jnp.float32)
        return carry

    for k in range(6):
        start = levels // SUB * SUB
        consts[k, pl.ds(start, pad - start), :] = jnp.full(
            (pad - start, LANES), 1.0 if k == 3 else 0.0, jnp.float32
        )
    lax.fori_loop(0, levels, fill, 0)
    consts[6] = LATENT / consts[3]
    for f in range(4):
        for h in range(halves):
            nat[f, h, pl.ds(used, (pad - levels) * rows), :] = jnp.zeros(
                ((pad - levels) * rows, LANES), jnp.float32
            )

    for k in list(range(3 * halves)) + [4 * halves, 4 * halves + 1]:
        loads[k].wait()

    def turn(i):
        for f in range(3):
            for h in range(halves):
                grid[i + 2, pl.ds(f * pad, pad), pl.ds(h * LANES, LANES)] = nat[
                    f, h, pl.ds(i, pad, stride=rows), :
                ]
        for k in range(3):
            grid[i + 2, pl.ds(levels + k, 1), pl.ds(0, cols)] = weights[k, pl.ds(i, 1), :]
        grid[i + 2, pl.ds(levels + 3, 1), pl.ds(0, cols)] = areas[pl.ds(i, 1), :]

    def turn_edge(n, carry):
        turn(n + n // 2 * (rows - 4))
        return carry

    lax.fori_loop(0, 4, turn_edge, 0)
    pl.semaphore_wait(barrier, len(greeted))

    sends = []

    def send(source, target, to):
        k = len(sends)
        copy = pltpu.make_async_remote_copy(
            src_ref=source,
            dst_ref=target,
            send_sem=send_sem.at[k],
            recv_sem=recv_sem.at[k],
            device_id=to,
            device_id_type=MESH,
        )
        copy.start()
        sends.append(copy)

    def send_rows(first, count):
        part = pl.ds(first, count)
        lanes = pl.ds(0, cols)
        send(grid.at[pl.ds(rows, 2), part, lanes], grid.at[pl.ds(0, 2), part, lanes], device(1, 0))
        send(
            grid.at[pl.ds(2, 2), part, lanes],
            grid.at[pl.ds(rows + 2, 2), part, lanes],
            device(-1, 0),
        )

    send_rows(0, 2 * pad)

    def turn_inner(n, carry):
        turn(n + 2)
        return carry

    lax.fori_loop(0, rows - 4, turn_inner, 0)

    lane = lax.broadcasted_iota(jnp.int32, (SUB, LANES), 1)
    per = LANES // (2 * rows)

    def edge_tile(r, g, dy):
        first = cols - LANES if dy > 0 else 0
        return grid[r, pl.ds(pl.multiple_of(g * SUB, SUB), SUB), pl.ds(first, LANES)]

    def pack(q, carry):
        for side, dy in enumerate((1, -1)):
            packed = jnp.zeros((SUB, LANES), jnp.float32)
            for part in range(per):
                for i in range(rows):
                    p = (part * rows + i) * 2
                    shift = (p - (LANES - 2 if dy > 0 else 0)) % LANES
                    moved = edge_tile(i + 2, q * per + part, dy)
                    if shift:
                        moved = pltpu.roll(moved, shift, 1)
                    packed = jnp.where(lane // 2 == p // 2, moved, packed)
            col_send[side, pl.ds(pl.multiple_of(q * SUB, SUB), SUB), :] = packed
        return carry

    lax.fori_loop(0, groups // per, pack, 0)
    send(col_send.at[0], col_recv.at[0], device(0, 1))
    send(col_send.at[1], col_recv.at[1], device(0, -1))

    def pack_corner(g, carry):
        result = []
        for (dx, dy), packed in zip(CORNERS, carry):
            for k in range(2):
                p = 4 * g + 2 * k
                moved = edge_tile((rows if dx > 0 else 2) + k, g, dy)
                moved = pltpu.roll(moved, lax.rem(p + (2 if dy > 0 else 0), LANES), 1)
                packed = jnp.where(lane // 2 == 2 * g + k, moved, packed)
            result.append(packed)
        return tuple(result)

    packed = lax.fori_loop(
        0, groups, pack_corner, tuple(jnp.zeros((SUB, LANES), jnp.float32) for _ in CORNERS)
    )
    for k, (dx, dy) in enumerate(CORNERS):
        corner_send[k] = packed[k]
        send(corner_send.at[k], corner_recv.at[k], device(dx, dy))
    send_rows(2 * pad, pad)

    loads[4 * halves + 2].wait()
    high_count = high.shape[0]

    def upper(i, carry):
        place = spans[pl.ds(i, 1), :] // LANES
        rank = lax.broadcasted_iota(jnp.int32, (high_count, cols), 0)
        hit = jnp.where(rank == place, 1.0, 0.0).astype(jnp.bfloat16)
        high[:, pl.ds(pl.multiple_of(i * cols, cols), cols)] = hit
        return carry

    lax.fori_loop(0, rows, upper, 0)

    sends[2].wait_recv()
    sends[3].wait_recv()

    def unpack(q, carry):
        at = pl.ds(pl.multiple_of(q * SUB, SUB), SUB)
        from_left = col_recv[0, at, :]
        from_right = col_recv[1, at, :]
        for part in range(per):
            for i in range(rows):
                p = (part * rows + i) * 2
                left = pltpu.roll(from_left, (LANES - 2 - p) % LANES, 1) if p != LANES - 2 else from_left
                right = pltpu.roll(from_right, (LANES - p) % LANES, 1) if p else from_right
                g = q * per + part
                grid[i + 2, pl.ds(pl.multiple_of(g * SUB, SUB), SUB), pl.ds(cols, LANES)] = jnp.where(
                    lane < 64, right, left
                )
        return carry

    lax.fori_loop(0, groups // per, unpack, 0)

    def laplace_at(source, r, at, c):
        up = source[r + 1, at, :]
        mid = source[r, at, :]
        down = source[r - 1, at, :]
        from_right = c[3] * mid + c[4] * down
        from_left = c[5] * mid + c[6] * up
        return (
            (c[0] * up + c[1] * down)
            + c[2] * mid
            + pltpu.roll(from_right, wide - 1, 1)
            + pltpu.roll(from_left, 1, 1)
        )

    def geometry(r, k):
        return jnp.broadcast_to(grid[r, pl.ds(levels + k, 1), :], (SUB, wide))

    def first_laplace(r):
        area = geometry(r, 3)
        area_right = pltpu.roll(area, wide - 1, 1)
        ahead = area * geometry(r, 0)
        behind = area * geometry(r - 1, 0)
        to_right = area * geometry(r, 1)
        to_right_behind = area * geometry(r, 2)
        own = geometry(r, 1)
        ahead_own = geometry(r + 1, 2)
        to_left = area_right * own
        to_left_ahead = area_right * ahead_own
        centre = -(
            ahead
            + behind
            + to_right
            + to_right_behind
            + pltpu.roll(to_left, 1, 1)
            + pltpu.roll(to_left_ahead, 1, 1)
        )
        c = (
            ahead,
            behind,
            centre,
            pltpu.roll(to_right, 1, 1),
            pltpu.roll(to_right_behind, 1, 1),
            to_left,
            to_left_ahead,
        )
        for k in range(7):
            coef[r, k] = c[k]

        def step(q, carry):
            for k in range(2):
                at = pl.ds(pl.multiple_of((q * 2 + k) * SUB, SUB), SUB)
                lap[r, at, :] = laplace_at(grid, r, at, c)
            return carry

        lax.fori_loop(0, groups // 2, step, 0)

    def coefficients(r):
        return tuple(coef[r, k] for k in range(7))

    def spread(k, at):
        tile = consts[k, at, :]
        return jnp.concatenate([tile] * halves, axis=1)

    def damped(f, r, q, c):
        at = pl.ds(pl.multiple_of(f * pad + q * SUB, SUB), SUB)
        del4 = laplace_at(lap, r, at, c)[:, :cols]
        here = pl.ds(pl.multiple_of(q * SUB, SUB), SUB)
        return grid[r, at, pl.ds(0, cols)] - spread(f, here) * del4

    def put(k, r, q, value):
        for h in range(halves):
            out[k, h, pl.ds(q * (SUB * rows) + r - 2, SUB, stride=rows), :] = value[
                :, h * LANES : (h + 1) * LANES
            ]

    def physics(r):
        c = coefficients(r)

        def step(q, rain):
            here = pl.ds(pl.multiple_of(q * SUB, SUB), SUB)
            theta_dyn = damped(0, r, q, c)
            vapor_dyn = damped(1, r, q, c)
            cloud_now = jnp.concatenate(
                [
                    nat[3, h, pl.ds(q * (SUB * rows) + r - 2, SUB, stride=rows), :]
                    for h in range(halves)
                ],
                axis=1,
            )
            temper = theta_dyn * spread(3, here)
            scale = spread(4, here)
            condensed = jnp.zeros_like(temper)
            for repeat in range(NSAT):
                warmed = temper + LATENT * condensed if repeat else temper
                saturation = scale * jnp.exp(warmed)
                excess = vapor_dyn - condensed - saturation
                condensed = condensed + excess / (1.0 + LATENT * saturation)
            condensed = jnp.maximum(condensed, -cloud_now)
            put(0, r, q, theta_dyn + condensed * spread(6, here))
            put(1, r, q, vapor_dyn - condensed)
            liquid = cloud_now + condensed
            rained = AUTO_RATE * jnp.maximum(liquid - QCRIT, 0.0)
            put(2, r, q, liquid - rained)
            return rain + spread(5, here) * rained

        rain = lax.fori_loop(0, pad // SUB, step, jnp.zeros((SUB, cols), jnp.float32))
        total = jnp.sum(rain, axis=0, keepdims=True)
        place = lax.rem(spans[pl.ds(r - 2, 1), :], LANES)
        rank = lax.broadcasted_iota(jnp.int32, (LANES, cols), 0)
        head = total.astype(jnp.bfloat16).astype(jnp.float32)
        at = pl.ds(pl.multiple_of((r - 2) * cols, cols), cols)
        for k, piece in enumerate((head, total - head)):
            low[pl.ds(k * LANES, LANES), at] = jnp.where(rank == place, piece, 0.0).astype(
                jnp.bfloat16
            )

    def loop(lower, upper_end, do):
        def step(r, carry):
            do(r)
            return carry

        lax.fori_loop(lower, upper_end, step, 0)

    loop(3, rows + 1, first_laplace)
    for h in range(halves):
        loads[3 * halves + h].wait()
    loop(4, rows, physics)

    for k in (0, 1, 4, 5, 6, 7, 8, 9):
        sends[k].wait_recv()

    def unpack_corner(g, carry):
        at = pl.ds(pl.multiple_of(g * SUB, SUB), SUB)
        for dx in (1, -1):
            for k in range(2):
                p = 4 * g + 2 * k
                left = corner_recv[CORNERS.index((dx, 1))]
                right = corner_recv[CORNERS.index((dx, -1))]
                left = pltpu.roll(left, lax.rem(2 * LANES - 2 - p, LANES), 1)
                right = pltpu.roll(right, lax.rem(LANES - p, LANES), 1)
                r = k if dx > 0 else rows + 2 + k
                grid[r, at, pl.ds(cols, LANES)] = jnp.where(lane < 64, right, left)
        return carry

    lax.fori_loop(0, groups, unpack_corner, 0)
    loop(0, 4, lambda n: first_laplace(n + 1 + n // 2 * (rows - 2)))
    loop(0, 4, lambda n: physics(n + 2 + n // 2 * (rows - 4)))

    both = lax.dot_general(
        high[...],
        low[...],
        (((1,), (1,)), ((), ())),
        preferred_element_type=jnp.float32,
    )
    rain_send[...] = both[:, :LANES] + both[:, LANES:]
    rains = []
    for d in range(1, n_py):
        to = device(0, d)
        copy = pltpu.make_async_remote_copy(
            src_ref=rain_send.at[pl.ds(pl.multiple_of(to[1] * block, block), block), :],
            dst_ref=rain_recv.at[d - 1],
            send_sem=rain_send_sem.at[d - 1],
            recv_sem=rain_recv_sem.at[d - 1],
            device_id=to,
            device_id_type=MESH,
        )
        copy.start()
        rains.append(copy)

    stores = []

    def store(k, target):
        for h in range(halves):
            copy = pltpu.make_async_copy(
                out.at[k, h, pl.ds(0, used), :],
                target.at[:, pl.ds(h * LANES, LANES)],
                out_sem.at[len(stores)],
            )
            copy.start()
            stores.append(copy)

    store(0, theta_out)
    store(1, vapor_out)
    store(2, cloud_out)

    def diverge(r):
        c = coefficients(r)

        def step(q, carry):
            put(3, r, q, damped(2, r, q, c))
            return carry

        lax.fori_loop(0, pad // SUB, step, 0)

    loop(2, rows + 2, diverge)
    store(3, divergence_out)

    total = rain_send[pl.ds(pl.multiple_of(py * block, block), block), :]
    for d in range(1, n_py):
        rains[d - 1].wait_recv()
        total = total + rain_recv[d - 1]
    precip_out[...] = total
    for copy in sends:
        copy.wait_send()
    for copy in rains:
        copy.wait_send()
    for copy in stores:
        copy.wait()


def on_device(
    n_px,
    n_py,
    theta,
    vapor,
    cloud,
    divergence,
    edge_weight,
    inv_area,
    damping,
    exner,
    sat_scale,
    layer_mass,
    span_of,
):
    levels, rows, cols = theta.shape
    pad = (levels + 4 + SUB - 1) // SUB * SUB
    halves = cols // LANES
    wide = cols + LANES
    block = rows * cols // LANES
    flat = jax.ShapeDtypeStruct((levels * rows, cols), jnp.float32)
    f32 = jnp.float32
    anywhere = pl.BlockSpec(memory_space=pl.ANY)
    scalars = pl.BlockSpec(memory_space=pltpu.SMEM)
    theta_next, vapor_next, cloud_next, divergence_next, precip = pl.pallas_call(
        functools.partial(kernel, (n_px, n_py, levels, rows, cols)),
        out_shape=(flat, flat, flat, flat, jax.ShapeDtypeStruct((block, LANES), f32)),
        in_specs=[anywhere] * 7 + [scalars] * 4,
        out_specs=(anywhere,) * 4 + (pl.BlockSpec(memory_space=pltpu.VMEM),),
        scratch_shapes=[
            pltpu.VMEM((4, halves, pad * rows, LANES), f32),
            pltpu.VMEM((4, halves, pad * rows, LANES), f32),
            pltpu.VMEM((rows + 4, 3 * pad, wide), f32),
            pltpu.VMEM((rows + 4, 3 * pad, wide), f32),
            pltpu.VMEM((rows + 4, 7, SUB, wide), f32),
            pltpu.VMEM((7, pad, LANES), f32),
            pltpu.VMEM((3, rows, cols), f32),
            pltpu.VMEM((rows, cols), f32),
            pltpu.VMEM((rows, cols), jnp.int32),
            pltpu.VMEM((2, 3 * pad * 2 * rows // LANES, LANES), f32),
            pltpu.VMEM((2, 3 * pad * 2 * rows // LANES, LANES), f32),
            pltpu.VMEM((4, SUB, LANES), f32),
            pltpu.VMEM((4, SUB, LANES), f32),
            pltpu.VMEM((n_py * block, rows * cols), jnp.bfloat16),
            pltpu.VMEM((2 * LANES, rows * cols), jnp.bfloat16),
            pltpu.VMEM((n_py * block, LANES), f32),
            pltpu.VMEM((n_py - 1, block, LANES), f32),
            pltpu.SemaphoreType.DMA((4 * halves + 3,)),
            pltpu.SemaphoreType.DMA((4 * halves,)),
            pltpu.SemaphoreType.DMA((10,)),
            pltpu.SemaphoreType.DMA((10,)),
            pltpu.SemaphoreType.DMA((n_py - 1,)),
            pltpu.SemaphoreType.DMA((n_py - 1,)),
        ],
        compiler_params=pltpu.CompilerParams(
            collective_id=0, has_side_effects=True, vmem_limit_bytes=48 * 1024 * 1024
        ),
        cost_estimate=pl.CostEstimate(
            flops=60 * levels * rows * cols, bytes_accessed=32 * levels * rows * cols, transcendentals=0
        ),
    )(
        theta.reshape(levels * rows, cols),
        vapor.reshape(levels * rows, cols),
        divergence.reshape(levels * rows, cols),
        cloud.reshape(levels * rows, cols),
        edge_weight,
        inv_area,
        span_of,
        damping,
        exner,
        sat_scale,
        layer_mass,
    )
    shape = (levels, rows, cols)
    return (
        theta_next.reshape(shape),
        vapor_next.reshape(shape),
        cloud_next.reshape(shape),
        divergence_next.reshape(shape),
        precip.reshape(1, block * LANES),
    )


def solution(mesh):
    placed = (
        P(None, "px", "py"),
        P(None, "px", "py"),
        P(None, "px", "py"),
        P(None, "px", "py"),
        P(None, "px", "py"),
        P("px", "py"),
        P(),
        P(),
        P(),
        P(),
        P("px", "py"),
    )
    return jax.shard_map(
        functools.partial(on_device, mesh.shape["px"], mesh.shape["py"]),
        mesh=mesh,
        in_specs=placed,
        out_specs=(
            P(None, "px", "py"),
            P(None, "px", "py"),
            P(None, "px", "py"),
            P(None, "px", "py"),
            P("px", "py"),
        ),
        check_vma=False,
    )
```

```python
import functools

import jax
import jax.numpy as jnp
from jax import lax
from jax.experimental import pallas as pl
from jax.experimental.pallas import tpu as pltpu
from jax.sharding import PartitionSpec as P

NSAT = 2
LATENT = 0.5
QCRIT = 0.2
AUTO_RATE = 0.5

MESH = pl.DeviceIdType.MESH
LANES = 128
SUB = 8
CORNERS = ((1, 1), (1, -1), (-1, 1), (-1, -1))


def kernel(
    dims,
    theta,
    vapor,
    divergence,
    cloud,
    edge_weight,
    inv_area,
    span_of,
    damping,
    exner,
    sat_scale,
    layer_mass,
    theta_out,
    vapor_out,
    cloud_out,
    divergence_out,
    precip_out,
    nat,
    out,
    grid,
    lap,
    coef,
    consts,
    weights,
    areas,
    spans,
    col_send,
    col_recv,
    corner_send,
    corner_recv,
    high,
    low,
    rain_rows,
    rain_send,
    rain_recv,
    in_sem,
    out_sem,
    send_sem,
    recv_sem,
    rain_send_sem,
    rain_recv_sem,
):
    n_px, n_py, levels, rows, cols = dims
    pad = consts.shape[1]
    halves = cols // LANES
    groups = 3 * pad // SUB
    wide = cols + LANES
    block = rows * cols // LANES
    px = lax.axis_index("px")
    py = lax.axis_index("py")
    used = levels * rows

    def device(dx, dy):
        return (lax.rem(px + dx + n_px, n_px), lax.rem(py + dy + n_py, n_py))

    loads = []
    for f, source in enumerate((theta, vapor, divergence, cloud)):
        for h in range(halves):
            loads.append(
                pltpu.make_async_copy(
                    source.at[:, pl.ds(h * LANES, LANES)],
                    nat.at[f, h, pl.ds(0, used), :],
                    in_sem.at[len(loads)],
                )
            )
    for source, target in ((edge_weight, weights), (inv_area, areas), (span_of, spans)):
        loads.append(pltpu.make_async_copy(source, target, in_sem.at[len(loads)]))
    for load in loads:
        load.start()

    barrier = pltpu.get_barrier_semaphore()
    greeted = [(1, 0), (-1, 0)] + list(CORNERS) + [(0, d) for d in range(1, n_py)]
    for dx, dy in greeted:
        pl.semaphore_signal(barrier, inc=1, device_id=device(dx, dy), device_id_type=MESH)

    def fill(level, carry):
        at = pl.ds(level, 1)
        for k in range(3):
            consts[k, at, :] = jnp.full((1, LANES), damping[k, level], jnp.float32)
        consts[3, at, :] = jnp.full((1, LANES), exner[level], jnp.float32)
        consts[4, at, :] = jnp.full((1, LANES), sat_scale[level], jnp.float32)
        consts[5, at, :] = jnp.full((1, LANES), layer_mass[level], jnp.float32)
        return carry

    for k in range(6):
        start = levels // SUB * SUB
        consts[k, pl.ds(start, pad - start), :] = jnp.full(
            (pad - start, LANES), 1.0 if k == 3 else 0.0, jnp.float32
        )
    lax.fori_loop(0, levels, fill, 0)
    consts[6] = LATENT / consts[3]
    for f in range(4):
        for h in range(halves):
            nat[f, h, pl.ds(used, (pad - levels) * rows), :] = jnp.zeros(
                ((pad - levels) * rows, LANES), jnp.float32
            )

    for k in list(range(3 * halves)) + [4 * halves, 4 * halves + 1]:
        loads[k].wait()

    def turn(i):
        for f in range(3):
            for h in range(halves):
                grid[i + 2, pl.ds(f * pad, pad), pl.ds(h * LANES, LANES)] = nat[
                    f, h, pl.ds(i, pad, stride=rows), :
                ]
        for k in range(3):
            grid[i + 2, pl.ds(levels + k, 1), pl.ds(0, cols)] = weights[k, pl.ds(i, 1), :]
        grid[i + 2, pl.ds(levels + 3, 1), pl.ds(0, cols)] = areas[pl.ds(i, 1), :]

    def turn_edge(n, carry):
        turn(n + n // 2 * (rows - 4))
        return carry

    lax.fori_loop(0, 4, turn_edge, 0)
    pl.semaphore_wait(barrier, len(greeted))

    sends = []

    def send(source, target, to):
        k = len(sends)
        copy = pltpu.make_async_remote_copy(
            src_ref=source,
            dst_ref=target,
            send_sem=send_sem.at[k],
            recv_sem=recv_sem.at[k],
            device_id=to,
            device_id_type=MESH,
        )
        copy.start()
        sends.append(copy)

    def send_rows(first, count):
        part = pl.ds(first, count)
        lanes = pl.ds(0, cols)
        send(grid.at[pl.ds(rows, 2), part, lanes], grid.at[pl.ds(0, 2), part, lanes], device(1, 0))
        send(
            grid.at[pl.ds(2, 2), part, lanes],
            grid.at[pl.ds(rows + 2, 2), part, lanes],
            device(-1, 0),
        )

    send_rows(0, 2 * pad)

    def turn_inner(n, carry):
        turn(n + 2)
        return carry

    lax.fori_loop(0, rows - 4, turn_inner, 0)

    lane = lax.broadcasted_iota(jnp.int32, (SUB, LANES), 1)
    per = LANES // (2 * rows)

    def edge_tile(r, g, dy):
        first = cols - LANES if dy > 0 else 0
        at = g * SUB if isinstance(g, int) else pl.multiple_of(g * SUB, SUB)
        return grid[r, pl.ds(at, SUB), pl.ds(first, LANES)]

    def pack(q, carry):
        for side, dy in enumerate((1, -1)):
            packed = jnp.zeros((SUB, LANES), jnp.float32)
            for part in range(per):
                for i in range(rows):
                    p = (part * rows + i) * 2
                    shift = (p - (LANES - 2 if dy > 0 else 0)) % LANES
                    moved = edge_tile(i + 2, q * per + part, dy)
                    if shift:
                        moved = pltpu.roll(moved, shift, 1)
                    packed = jnp.where(lane // 2 == p // 2, moved, packed)
            col_send[side, pl.ds(pl.multiple_of(q * SUB, SUB), SUB), :] = packed
        return carry

    lax.fori_loop(0, groups // per, pack, 0)
    send(col_send.at[0], col_recv.at[0], device(0, 1))
    send(col_send.at[1], col_recv.at[1], device(0, -1))

    pair = lane // 2
    for n, (dx, dy) in enumerate(CORNERS):
        packed = jnp.zeros((SUB, LANES), jnp.float32)
        for g in range(groups):
            for k in range(2):
                p = 4 * g + 2 * k
                moved = edge_tile((rows if dx > 0 else 2) + k, g, dy)
                shift = (p + (2 if dy > 0 else 0)) % LANES
                if shift:
                    moved = pltpu.roll(moved, shift, 1)
                packed = jnp.where(pair == p // 2, moved, packed)
        corner_send[n] = packed
        send(corner_send.at[n], corner_recv.at[n], device(dx, dy))
    send_rows(2 * pad, pad)

    loads[4 * halves + 2].wait()
    high_count = high.shape[0]

    def upper(i, carry):
        place = spans[pl.ds(i, 1), :] // LANES
        rank = lax.broadcasted_iota(jnp.int32, (high_count, cols), 0)
        hit = jnp.where(rank == place, 1.0, 0.0).astype(jnp.bfloat16)
        high[:, pl.ds(pl.multiple_of(i * cols, cols), cols)] = hit
        return carry

    lax.fori_loop(0, rows, upper, 0)

    sends[2].wait_recv()
    sends[3].wait_recv()

    def unpack(q, carry):
        at = pl.ds(pl.multiple_of(q * SUB, SUB), SUB)
        from_left = col_recv[0, at, :]
        from_right = col_recv[1, at, :]
        for part in range(per):
            for i in range(rows):
                p = (part * rows + i) * 2
                left = pltpu.roll(from_left, (LANES - 2 - p) % LANES, 1) if p != LANES - 2 else from_left
                right = pltpu.roll(from_right, (LANES - p) % LANES, 1) if p else from_right
                g = q * per + part
                grid[i + 2, pl.ds(pl.multiple_of(g * SUB, SUB), SUB), pl.ds(cols, LANES)] = jnp.where(
                    lane < 64, right, left
                )
        return carry

    lax.fori_loop(0, groups // per, unpack, 0)

    def laplace_at(source, r, at, c):
        up = source[r + 1, at, :]
        mid = source[r, at, :]
        down = source[r - 1, at, :]
        from_right = c[3] * mid + c[4] * down
        from_left = c[5] * mid + c[6] * up
        return (
            (c[0] * up + c[1] * down)
            + c[2] * mid
            + pltpu.roll(from_right, wide - 1, 1)
            + pltpu.roll(from_left, 1, 1)
        )

    def geometry(r, k):
        return jnp.broadcast_to(grid[r, pl.ds(levels + k, 1), :], (SUB, wide))

    def first_laplace(r):
        area = geometry(r, 3)
        area_right = pltpu.roll(area, wide - 1, 1)
        ahead = area * geometry(r, 0)
        behind = area * geometry(r - 1, 0)
        to_right = area * geometry(r, 1)
        to_right_behind = area * geometry(r, 2)
        own = geometry(r, 1)
        ahead_own = geometry(r + 1, 2)
        to_left = area_right * own
        to_left_ahead = area_right * ahead_own
        centre = -(
            ahead
            + behind
            + to_right
            + to_right_behind
            + pltpu.roll(to_left, 1, 1)
            + pltpu.roll(to_left_ahead, 1, 1)
        )
        c = (
            ahead,
            behind,
            centre,
            pltpu.roll(to_right, 1, 1),
            pltpu.roll(to_right_behind, 1, 1),
            to_left,
            to_left_ahead,
        )
        for k in range(7):
            coef[r, k] = c[k]

        for g in range(groups):
            at = pl.ds(g * SUB, SUB)
            lap[r, at, :] = laplace_at(grid, r, at, c)

    def coefficients(r):
        return tuple(coef[r, k] for k in range(7))

    def spread(k, at):
        tile = consts[k, at, :]
        return jnp.concatenate([tile] * halves, axis=1)

    def damped(f, r, q, c):
        at = pl.ds(f * pad + q * SUB, SUB)
        del4 = laplace_at(lap, r, at, c)[:, :cols]
        here = pl.ds(q * SUB, SUB)
        return grid[r, at, pl.ds(0, cols)] - spread(f, here) * del4

    def put(k, r, q, value):
        for h in range(halves):
            out[k, h, pl.ds(q * (SUB * rows) + r - 2, SUB, stride=rows), :] = value[
                :, h * LANES : (h + 1) * LANES
            ]

    def physics(r):
        c = coefficients(r)

        rain = jnp.zeros((SUB, cols), jnp.float32)
        for q in range(pad // SUB):
            here = pl.ds(q * SUB, SUB)
            theta_dyn = damped(0, r, q, c)
            vapor_dyn = damped(1, r, q, c)
            cloud_now = jnp.concatenate(
                [
                    nat[3, h, pl.ds(q * (SUB * rows) + r - 2, SUB, stride=rows), :]
                    for h in range(halves)
                ],
                axis=1,
            )
            temper = theta_dyn * spread(3, here)
            scale = spread(4, here)
            condensed = jnp.zeros_like(temper)
            for repeat in range(NSAT):
                warmed = temper + LATENT * condensed if repeat else temper
                saturation = scale * jnp.exp(warmed)
                excess = vapor_dyn - condensed - saturation
                condensed = condensed + excess / (1.0 + LATENT * saturation)
            condensed = jnp.maximum(condensed, -cloud_now)
            put(0, r, q, theta_dyn + condensed * spread(6, here))
            put(1, r, q, vapor_dyn - condensed)
            liquid = cloud_now + condensed
            rained = AUTO_RATE * jnp.maximum(liquid - QCRIT, 0.0)
            put(2, r, q, liquid - rained)
            rain = rain + spread(5, here) * rained
        rain_rows[r - 2] = rain

    rank_low = lax.broadcasted_iota(jnp.int32, (LANES, cols), 0)

    def lower(i):
        total = jnp.sum(rain_rows[i], axis=0, keepdims=True)
        place = lax.rem(spans[pl.ds(i, 1), :], LANES)
        head = total.astype(jnp.bfloat16).astype(jnp.float32)
        at = pl.ds(pl.multiple_of(i * cols, cols), cols)
        hit = rank_low == place
        for k, piece in enumerate((head, total - head)):
            low[pl.ds(k * LANES, LANES), at] = jnp.where(hit, piece, 0.0).astype(jnp.bfloat16)

    def product(first, count):
        at = pl.ds(first * cols, count * cols)
        both = lax.dot_general(
            high[:, at], low[:, at], (((1,), (1,)), ((), ())), preferred_element_type=jnp.float32
        )
        return both[:, :LANES] + both[:, LANES:]

    def loop(first, end, do):
        def step(r, carry):
            do(r)
            return carry

        lax.fori_loop(first, end, step, 0)

    loop(3, rows + 1, first_laplace)
    for h in range(halves):
        loads[3 * halves + h].wait()
    loop(4, rows, physics)
    loop(2, rows - 2, lower)
    rain_send[...] = product(2, rows - 4)

    for k in (0, 1, 4, 5, 6, 7, 8, 9):
        sends[k].wait_recv()

    for dx in (1, -1):
        for g in range(groups):
            for k in range(2):
                p = 4 * g + 2 * k
                left = corner_recv[CORNERS.index((dx, 1))]
                right = corner_recv[CORNERS.index((dx, -1))]
                left = pltpu.roll(left, (LANES - 2 - p) % LANES, 1) if p != LANES - 2 else left
                right = pltpu.roll(right, LANES - p, 1) if p else right
                r = k if dx > 0 else rows + 2 + k
                grid[r, pl.ds(g * SUB, SUB), pl.ds(cols, LANES)] = jnp.where(lane < 64, right, left)
    loop(0, 4, lambda n: first_laplace(n + 1 + n // 2 * (rows - 2)))
    loop(0, 4, lambda n: physics(n + 2 + n // 2 * (rows - 4)))

    for i in (0, 1, rows - 2, rows - 1):
        lower(i)

    rain_send[...] += product(0, 2) + product(rows - 2, 2)
    rains = []
    for d in range(1, n_py):
        to = device(0, d)
        copy = pltpu.make_async_remote_copy(
            src_ref=rain_send.at[pl.ds(pl.multiple_of(to[1] * block, block), block), :],
            dst_ref=rain_recv.at[d - 1],
            send_sem=rain_send_sem.at[d - 1],
            recv_sem=rain_recv_sem.at[d - 1],
            device_id=to,
            device_id_type=MESH,
        )
        copy.start()
        rains.append(copy)

    stores = []

    def store(k, target):
        for h in range(halves):
            copy = pltpu.make_async_copy(
                out.at[k, h, pl.ds(0, used), :],
                target.at[:, pl.ds(h * LANES, LANES)],
                out_sem.at[len(stores)],
            )
            copy.start()
            stores.append(copy)

    store(0, theta_out)
    store(1, vapor_out)
    store(2, cloud_out)

    def diverge(r):
        c = coefficients(r)
        for q in range(pad // SUB):
            put(3, r, q, damped(2, r, q, c))

    loop(2, rows + 2, diverge)
    store(3, divergence_out)

    total = rain_send[pl.ds(pl.multiple_of(py * block, block), block), :]
    for d in range(1, n_py):
        rains[d - 1].wait_recv()
        total = total + rain_recv[d - 1]
    precip_out[...] = total
    for copy in sends:
        copy.wait_send()
    for copy in rains:
        copy.wait_send()
    for copy in stores:
        copy.wait()


def on_device(
    n_px,
    n_py,
    theta,
    vapor,
    cloud,
    divergence,
    edge_weight,
    inv_area,
    damping,
    exner,
    sat_scale,
    layer_mass,
    span_of,
):
    levels, rows, cols = theta.shape
    pad = (levels + 4 + SUB - 1) // SUB * SUB
    halves = cols // LANES
    wide = cols + LANES
    block = rows * cols // LANES
    flat = jax.ShapeDtypeStruct((levels * rows, cols), jnp.float32)
    f32 = jnp.float32
    anywhere = pl.BlockSpec(memory_space=pl.ANY)
    scalars = pl.BlockSpec(memory_space=pltpu.SMEM)
    theta_next, vapor_next, cloud_next, divergence_next, precip = pl.pallas_call(
        functools.partial(kernel, (n_px, n_py, levels, rows, cols)),
        out_shape=(flat, flat, flat, flat, jax.ShapeDtypeStruct((block, LANES), f32)),
        in_specs=[anywhere] * 7 + [scalars] * 4,
        out_specs=(anywhere,) * 4 + (pl.BlockSpec(memory_space=pltpu.VMEM),),
        scratch_shapes=[
            pltpu.VMEM((4, halves, pad * rows, LANES), f32),
            pltpu.VMEM((4, halves, pad * rows, LANES), f32),
            pltpu.VMEM((rows + 4, 3 * pad, wide), f32),
            pltpu.VMEM((rows + 4, 3 * pad, wide), f32),
            pltpu.VMEM((rows + 4, 7, SUB, wide), f32),
            pltpu.VMEM((7, pad, LANES), f32),
            pltpu.VMEM((3, rows, cols), f32),
            pltpu.VMEM((rows, cols), f32),
            pltpu.VMEM((rows, cols), jnp.int32),
            pltpu.VMEM((2, 3 * pad * 2 * rows // LANES, LANES), f32),
            pltpu.VMEM((2, 3 * pad * 2 * rows // LANES, LANES), f32),
            pltpu.VMEM((4, SUB, LANES), f32),
            pltpu.VMEM((4, SUB, LANES), f32),
            pltpu.VMEM((n_py * block, rows * cols), jnp.bfloat16),
            pltpu.VMEM((2 * LANES, rows * cols), jnp.bfloat16),
            pltpu.VMEM((rows, SUB, cols), f32),
            pltpu.VMEM((n_py * block, LANES), f32),
            pltpu.VMEM((n_py - 1, block, LANES), f32),
            pltpu.SemaphoreType.DMA((4 * halves + 3,)),
            pltpu.SemaphoreType.DMA((4 * halves,)),
            pltpu.SemaphoreType.DMA((10,)),
            pltpu.SemaphoreType.DMA((10,)),
            pltpu.SemaphoreType.DMA((n_py - 1,)),
            pltpu.SemaphoreType.DMA((n_py - 1,)),
        ],
        compiler_params=pltpu.CompilerParams(
            collective_id=0, has_side_effects=True, vmem_limit_bytes=60 * 1024 * 1024
        ),
        cost_estimate=pl.CostEstimate(
            flops=60 * levels * rows * cols, bytes_accessed=32 * levels * rows * cols, transcendentals=0
        ),
    )(
        theta.reshape(levels * rows, cols),
        vapor.reshape(levels * rows, cols),
        divergence.reshape(levels * rows, cols),
        cloud.reshape(levels * rows, cols),
        edge_weight,
        inv_area,
        span_of,
        damping,
        exner,
        sat_scale,
        layer_mass,
    )
    shape = (levels, rows, cols)
    return (
        theta_next.reshape(shape),
        vapor_next.reshape(shape),
        cloud_next.reshape(shape),
        divergence_next.reshape(shape),
        precip.reshape(1, block * LANES),
    )


def solution(mesh):
    placed = (
        P(None, "px", "py"),
        P(None, "px", "py"),
        P(None, "px", "py"),
        P(None, "px", "py"),
        P(None, "px", "py"),
        P("px", "py"),
        P(),
        P(),
        P(),
        P(),
        P("px", "py"),
    )
    return jax.shard_map(
        functools.partial(on_device, mesh.shape["px"], mesh.shape["py"]),
        mesh=mesh,
        in_specs=placed,
        out_specs=(
            P(None, "px", "py"),
            P(None, "px", "py"),
            P(None, "px", "py"),
            P(None, "px", "py"),
            P("px", "py"),
        ),
        check_vma=False,
    )
```

```python
import functools

import jax
import jax.numpy as jnp
from jax import lax
from jax.experimental import pallas as pl
from jax.experimental.pallas import tpu as pltpu
from jax.sharding import PartitionSpec as P

NSAT = 2
LATENT = 0.5
QCRIT = 0.2
AUTO_RATE = 0.5

MESH = pl.DeviceIdType.MESH
LANES = 128
SUB = 8
CORNERS = ((1, 1), (1, -1), (-1, 1), (-1, -1))


def kernel(
    dims,
    theta,
    vapor,
    divergence,
    cloud,
    edge_weight,
    inv_area,
    span_of,
    damping,
    exner,
    sat_scale,
    layer_mass,
    theta_out,
    vapor_out,
    cloud_out,
    divergence_out,
    precip_out,
    nat,
    out,
    grid,
    lap,
    coef,
    consts,
    weights,
    areas,
    spans,
    col_send,
    col_recv,
    corner_send,
    corner_recv,
    high,
    low,
    rain_rows,
    rain_send,
    rain_recv,
    in_sem,
    out_sem,
    send_sem,
    recv_sem,
    rain_send_sem,
    rain_recv_sem,
):
    n_px, n_py, levels, rows, cols = dims
    pad = consts.shape[1]
    halves = cols // LANES
    groups = 3 * pad // SUB
    wide = cols + LANES
    block = rows * cols // LANES
    px = lax.axis_index("px")
    py = lax.axis_index("py")
    used = levels * rows

    def device(dx, dy):
        return (lax.rem(px + dx + n_px, n_px), lax.rem(py + dy + n_py, n_py))

    loads = []
    for source, target in ((span_of, spans), (edge_weight, weights), (inv_area, areas)):
        loads.append(pltpu.make_async_copy(source, target, in_sem.at[len(loads)]))
    for f, source in enumerate((theta, vapor, divergence, cloud)):
        for h in range(halves):
            loads.append(
                pltpu.make_async_copy(
                    source.at[:, pl.ds(h * LANES, LANES)],
                    nat.at[f, h, pl.ds(0, used), :],
                    in_sem.at[len(loads)],
                )
            )
    for load in loads:
        load.start()

    barrier = pltpu.get_barrier_semaphore()
    greeted = [(1, 0), (-1, 0)] + list(CORNERS) + [(0, d) for d in range(1, n_py)]
    for dx, dy in greeted:
        pl.semaphore_signal(barrier, inc=1, device_id=device(dx, dy), device_id_type=MESH)

    def fill(level, carry):
        at = pl.ds(level, 1)
        for k in range(3):
            consts[k, at, :] = jnp.full((1, LANES), damping[k, level], jnp.float32)
        consts[3, at, :] = jnp.full((1, LANES), exner[level], jnp.float32)
        consts[4, at, :] = jnp.full((1, LANES), sat_scale[level], jnp.float32)
        consts[5, at, :] = jnp.full((1, LANES), layer_mass[level], jnp.float32)
        return carry

    for k in range(6):
        start = levels // SUB * SUB
        consts[k, pl.ds(start, pad - start), :] = jnp.full(
            (pad - start, LANES), 1.0 if k == 3 else 0.0, jnp.float32
        )
    lax.fori_loop(0, levels, fill, 0)
    consts[6] = LATENT / consts[3]
    for f in range(4):
        for h in range(halves):
            nat[f, h, pl.ds(used, (pad - levels) * rows), :] = jnp.zeros(
                ((pad - levels) * rows, LANES), jnp.float32
            )

    loads[0].wait()
    high_count = high.shape[0]

    def upper(i, carry):
        place = spans[pl.ds(i, 1), :] // LANES
        rank = lax.broadcasted_iota(jnp.int32, (high_count, cols), 0)
        hit = jnp.where(rank == place, 1.0, 0.0).astype(jnp.bfloat16)
        high[:, pl.ds(pl.multiple_of(i * cols, cols), cols)] = hit
        return carry

    lax.fori_loop(0, rows, upper, 0)

    for load in loads[1 : 3 + 3 * halves]:
        load.wait()

    def turn(i):
        for f in range(3):
            for h in range(halves):
                grid[i + 2, pl.ds(f * pad, pad), pl.ds(h * LANES, LANES)] = nat[
                    f, h, pl.ds(i, pad, stride=rows), :
                ]
        for k in range(3):
            grid[i + 2, pl.ds(levels + k, 1), pl.ds(0, cols)] = weights[k, pl.ds(i, 1), :]
        grid[i + 2, pl.ds(levels + 3, 1), pl.ds(0, cols)] = areas[pl.ds(i, 1), :]

    def turn_edge(n, carry):
        turn(n + n // 2 * (rows - 4))
        return carry

    lax.fori_loop(0, 4, turn_edge, 0)
    pl.semaphore_wait(barrier, len(greeted))

    sends = []

    def send(source, target, to):
        k = len(sends)
        copy = pltpu.make_async_remote_copy(
            src_ref=source,
            dst_ref=target,
            send_sem=send_sem.at[k],
            recv_sem=recv_sem.at[k],
            device_id=to,
            device_id_type=MESH,
        )
        copy.start()
        sends.append(copy)

    def send_rows(first, count):
        part = pl.ds(first, count)
        lanes = pl.ds(0, cols)
        send(grid.at[pl.ds(rows, 2), part, lanes], grid.at[pl.ds(0, 2), part, lanes], device(1, 0))
        send(
            grid.at[pl.ds(2, 2), part, lanes],
            grid.at[pl.ds(rows + 2, 2), part, lanes],
            device(-1, 0),
        )

    send_rows(0, 2 * pad)

    def turn_inner(n, carry):
        turn(n + 2)
        return carry

    lax.fori_loop(0, rows - 4, turn_inner, 0)

    lane = lax.broadcasted_iota(jnp.int32, (SUB, LANES), 1)
    per = LANES // (2 * rows)

    def edge_tile(r, g, dy):
        first = cols - LANES if dy > 0 else 0
        at = g * SUB if isinstance(g, int) else pl.multiple_of(g * SUB, SUB)
        return grid[r, pl.ds(at, SUB), pl.ds(first, LANES)]

    def pack(q, carry):
        for side, dy in enumerate((1, -1)):
            packed = jnp.zeros((SUB, LANES), jnp.float32)
            for part in range(per):
                for i in range(rows):
                    p = (part * rows + i) * 2
                    shift = (p - (LANES - 2 if dy > 0 else 0)) % LANES
                    moved = edge_tile(i + 2, q * per + part, dy)
                    if shift:
                        moved = pltpu.roll(moved, shift, 1)
                    packed = jnp.where(lane // 2 == p // 2, moved, packed)
            col_send[side, pl.ds(pl.multiple_of(q * SUB, SUB), SUB), :] = packed
        return carry

    lax.fori_loop(0, groups // per, pack, 0)
    send(col_send.at[0], col_recv.at[0], device(0, 1))
    send(col_send.at[1], col_recv.at[1], device(0, -1))

    pair = lane // 2
    for n, (dx, dy) in enumerate(CORNERS):
        packed = jnp.zeros((SUB, LANES), jnp.float32)
        for g in range(groups):
            for k in range(2):
                p = 4 * g + 2 * k
                moved = edge_tile((rows if dx > 0 else 2) + k, g, dy)
                shift = (p + (2 if dy > 0 else 0)) % LANES
                if shift:
                    moved = pltpu.roll(moved, shift, 1)
                packed = jnp.where(pair == p // 2, moved, packed)
        corner_send[n] = packed
        send(corner_send.at[n], corner_recv.at[n], device(dx, dy))
    send_rows(2 * pad, pad)

    sends[2].wait_recv()
    sends[3].wait_recv()

    def unpack(q, carry):
        at = pl.ds(pl.multiple_of(q * SUB, SUB), SUB)
        from_left = col_recv[0, at, :]
        from_right = col_recv[1, at, :]
        for part in range(per):
            for i in range(rows):
                p = (part * rows + i) * 2
                left = pltpu.roll(from_left, (LANES - 2 - p) % LANES, 1) if p != LANES - 2 else from_left
                right = pltpu.roll(from_right, (LANES - p) % LANES, 1) if p else from_right
                g = q * per + part
                grid[i + 2, pl.ds(pl.multiple_of(g * SUB, SUB), SUB), pl.ds(cols, LANES)] = jnp.where(
                    lane < 64, right, left
                )
        return carry

    lax.fori_loop(0, groups // per, unpack, 0)

    def laplace_at(source, r, at, c):
        up = source[r + 1, at, :]
        mid = source[r, at, :]
        down = source[r - 1, at, :]
        from_right = c[3] * mid + c[4] * down
        from_left = c[5] * mid + c[6] * up
        return (
            (c[0] * up + c[1] * down)
            + c[2] * mid
            + pltpu.roll(from_right, wide - 1, 1)
            + pltpu.roll(from_left, 1, 1)
        )

    def geometry(r, k):
        return jnp.broadcast_to(grid[r, pl.ds(levels + k, 1), :], (SUB, wide))

    def first_laplace(r):
        area = geometry(r, 3)
        area_right = pltpu.roll(area, wide - 1, 1)
        ahead = area * geometry(r, 0)
        behind = area * geometry(r - 1, 0)
        to_right = area * geometry(r, 1)
        to_right_behind = area * geometry(r, 2)
        own = geometry(r, 1)
        ahead_own = geometry(r + 1, 2)
        to_left = area_right * own
        to_left_ahead = area_right * ahead_own
        centre = -(
            ahead
            + behind
            + to_right
            + to_right_behind
            + pltpu.roll(to_left, 1, 1)
            + pltpu.roll(to_left_ahead, 1, 1)
        )
        c = (
            ahead,
            behind,
            centre,
            pltpu.roll(to_right, 1, 1),
            pltpu.roll(to_right_behind, 1, 1),
            to_left,
            to_left_ahead,
        )
        for k in range(7):
            coef[r, k] = c[k]

        for g in range(2 * pad // SUB):
            at = pl.ds(g * SUB, SUB)
            lap[r, at, :] = laplace_at(grid, r, at, c)

    def coefficients(r):
        return tuple(coef[r, k] for k in range(7))

    def spread(k, at):
        tile = consts[k, at, :]
        return jnp.concatenate([tile] * halves, axis=1)

    def damped(f, r, q, c):
        at = pl.ds(f * pad + q * SUB, SUB)
        del4 = laplace_at(lap, r, at, c)[:, :cols]
        here = pl.ds(q * SUB, SUB)
        return grid[r, at, pl.ds(0, cols)] - spread(f, here) * del4

    def put(k, r, q, value):
        for h in range(halves):
            out[k, h, pl.ds(q * (SUB * rows) + r - 2, SUB, stride=rows), :] = value[
                :, h * LANES : (h + 1) * LANES
            ]

    def physics(r):
        c = coefficients(r)

        rain = jnp.zeros((SUB, cols), jnp.float32)
        for q in range(pad // SUB):
            here = pl.ds(q * SUB, SUB)
            theta_dyn = damped(0, r, q, c)
            vapor_dyn = damped(1, r, q, c)
            cloud_now = jnp.concatenate(
                [
                    nat[3, h, pl.ds(q * (SUB * rows) + r - 2, SUB, stride=rows), :]
                    for h in range(halves)
                ],
                axis=1,
            )
            temper = theta_dyn * spread(3, here)
            scale = spread(4, here)
            condensed = jnp.zeros_like(temper)
            for repeat in range(NSAT):
                warmed = temper + LATENT * condensed if repeat else temper
                saturation = scale * jnp.exp(warmed)
                excess = vapor_dyn - condensed - saturation
                condensed = condensed + excess / (1.0 + LATENT * saturation)
            condensed = jnp.maximum(condensed, -cloud_now)
            put(0, r, q, theta_dyn + condensed * spread(6, here))
            put(1, r, q, vapor_dyn - condensed)
            liquid = cloud_now + condensed
            rained = AUTO_RATE * jnp.maximum(liquid - QCRIT, 0.0)
            put(2, r, q, liquid - rained)
            rain = rain + spread(5, here) * rained
        rain_rows[r - 2] = rain

    rank_low = lax.broadcasted_iota(jnp.int32, (LANES, cols), 0)

    def lower(i):
        total = jnp.sum(rain_rows[i], axis=0, keepdims=True)
        place = lax.rem(spans[pl.ds(i, 1), :], LANES)
        head = total.astype(jnp.bfloat16).astype(jnp.float32)
        at = pl.ds(pl.multiple_of(i * cols, cols), cols)
        hit = rank_low == place
        for k, piece in enumerate((head, total - head)):
            low[pl.ds(k * LANES, LANES), at] = jnp.where(hit, piece, 0.0).astype(jnp.bfloat16)

    def product(first, count):
        at = pl.ds(first * cols, count * cols)
        both = lax.dot_general(
            high[:, at], low[:, at], (((1,), (1,)), ((), ())), preferred_element_type=jnp.float32
        )
        return both[:, :LANES] + both[:, LANES:]

    def loop(first, end, do):
        def step(r, carry):
            do(r)
            return carry

        lax.fori_loop(first, end, step, 0)

    loop(3, rows + 1, first_laplace)
    for h in range(halves):
        loads[3 + 3 * halves + h].wait()
    loop(4, rows, physics)

    def lower_four(n):
        for k in range(4):
            lower(2 + 4 * n + k)

    loop(0, (rows - 4) // 4, lower_four)
    rain_send[...] = product(2, rows - 4)

    for k in (0, 1, 4, 5, 6, 7):
        sends[k].wait_recv()

    for dx in (1, -1):
        for g in range(groups):
            for k in range(2):
                p = 4 * g + 2 * k
                left = corner_recv[CORNERS.index((dx, 1))]
                right = corner_recv[CORNERS.index((dx, -1))]
                left = pltpu.roll(left, (LANES - 2 - p) % LANES, 1) if p != LANES - 2 else left
                right = pltpu.roll(right, LANES - p, 1) if p else right
                r = k if dx > 0 else rows + 2 + k
                grid[r, pl.ds(g * SUB, SUB), pl.ds(cols, LANES)] = jnp.where(lane < 64, right, left)
    loop(0, 4, lambda n: first_laplace(n + 1 + n // 2 * (rows - 2)))
    loop(0, 4, lambda n: physics(n + 2 + n // 2 * (rows - 4)))

    for i in (0, 1, rows - 2, rows - 1):
        lower(i)

    rain_send[...] += product(0, 2) + product(rows - 2, 2)
    rains = []
    for d in range(1, n_py):
        to = device(0, d)
        copy = pltpu.make_async_remote_copy(
            src_ref=rain_send.at[pl.ds(pl.multiple_of(to[1] * block, block), block), :],
            dst_ref=rain_recv.at[d - 1],
            send_sem=rain_send_sem.at[d - 1],
            recv_sem=rain_recv_sem.at[d - 1],
            device_id=to,
            device_id_type=MESH,
        )
        copy.start()
        rains.append(copy)

    stores = []

    def store(k, target):
        for h in range(halves):
            copy = pltpu.make_async_copy(
                out.at[k, h, pl.ds(0, used), :],
                target.at[:, pl.ds(h * LANES, LANES)],
                out_sem.at[len(stores)],
            )
            copy.start()
            stores.append(copy)

    store(0, theta_out)
    store(1, vapor_out)
    store(2, cloud_out)

    for k in (8, 9):
        sends[k].wait_recv()

    def diverge_first(n):
        for r in (1 + 2 * n, 2 + 2 * n):
            c = coefficients(r)
            for g in range(2 * pad // SUB, groups):
                at = pl.ds(g * SUB, SUB)
                lap[r, at, :] = laplace_at(grid, r, at, c)

    def diverge(n):
        for r in (2 + 2 * n, 3 + 2 * n):
            c = coefficients(r)
            for q in range(pad // SUB):
                put(3, r, q, damped(2, r, q, c))

    loop(0, rows // 2 + 1, diverge_first)
    loop(0, rows // 2, diverge)
    store(3, divergence_out)

    total = rain_send[pl.ds(pl.multiple_of(py * block, block), block), :]
    for d in range(1, n_py):
        rains[d - 1].wait_recv()
        total = total + rain_recv[d - 1]
    precip_out[...] = total
    for copy in sends:
        copy.wait_send()
    for copy in rains:
        copy.wait_send()
    for copy in stores:
        copy.wait()


def placing(*refs):
    count = len(refs) // 2
    sem = refs[-1]
    copies = []
    for k in range(count):
        half = refs[k].shape[0] // 2
        for part in range(2):
            at = pl.ds(part * half, half)
            copies.append(
                pltpu.make_async_copy(refs[k].at[at], refs[count + k].at[at], sem.at[k, part])
            )
    for copy in copies:
        copy.start()
    for copy in copies:
        copy.wait()


def on_device(
    n_px,
    n_py,
    theta,
    vapor,
    cloud,
    divergence,
    edge_weight,
    inv_area,
    damping,
    exner,
    sat_scale,
    layer_mass,
    span_of,
):
    levels, rows, cols = theta.shape
    pad = (levels + 4 + SUB - 1) // SUB * SUB
    halves = cols // LANES
    wide = cols + LANES
    block = rows * cols // LANES
    flat = jax.ShapeDtypeStruct((levels * rows, cols), jnp.float32)
    f32 = jnp.float32
    anywhere = pl.BlockSpec(memory_space=pl.ANY)
    far = pl.BlockSpec(memory_space=pltpu.HBM)
    scalars = pl.BlockSpec(memory_space=pltpu.SMEM)
    made = pl.pallas_call(
        functools.partial(kernel, (n_px, n_py, levels, rows, cols)),
        out_shape=(flat, flat, flat, flat, jax.ShapeDtypeStruct((block, LANES), f32)),
        in_specs=[far] * 7 + [scalars] * 4,
        out_specs=(anywhere,) * 4 + (pl.BlockSpec(memory_space=pltpu.VMEM),),
        scratch_shapes=[
            pltpu.VMEM((4, halves, pad * rows, LANES), f32),
            pltpu.VMEM((4, halves, pad * rows, LANES), f32),
            pltpu.VMEM((rows + 4, 3 * pad, wide), f32),
            pltpu.VMEM((rows + 4, 3 * pad, wide), f32),
            pltpu.VMEM((rows + 4, 7, SUB, wide), f32),
            pltpu.VMEM((7, pad, LANES), f32),
            pltpu.VMEM((3, rows, cols), f32),
            pltpu.VMEM((rows, cols), f32),
            pltpu.VMEM((rows, cols), jnp.int32),
            pltpu.VMEM((2, 3 * pad * 2 * rows // LANES, LANES), f32),
            pltpu.VMEM((2, 3 * pad * 2 * rows // LANES, LANES), f32),
            pltpu.VMEM((4, SUB, LANES), f32),
            pltpu.VMEM((4, SUB, LANES), f32),
            pltpu.VMEM((n_py * block, rows * cols), jnp.bfloat16),
            pltpu.VMEM((2 * LANES, rows * cols), jnp.bfloat16),
            pltpu.VMEM((rows, SUB, cols), f32),
            pltpu.VMEM((n_py * block, LANES), f32),
            pltpu.VMEM((n_py - 1, block, LANES), f32),
            pltpu.SemaphoreType.DMA((4 * halves + 3,)),
            pltpu.SemaphoreType.DMA((4 * halves,)),
            pltpu.SemaphoreType.DMA((10,)),
            pltpu.SemaphoreType.DMA((10,)),
            pltpu.SemaphoreType.DMA((n_py - 1,)),
            pltpu.SemaphoreType.DMA((n_py - 1,)),
        ],
        compiler_params=pltpu.CompilerParams(
            collective_id=0, has_side_effects=True, vmem_limit_bytes=40 * 1024 * 1024
        ),
        cost_estimate=pl.CostEstimate(
            flops=60 * levels * rows * cols, bytes_accessed=32 * levels * rows * cols, transcendentals=0
        ),
    )(
        *[
            pltpu.with_memory_space_constraint(array, pltpu.HBM)
            for array in (
                theta.reshape(levels * rows, cols),
                vapor.reshape(levels * rows, cols),
                divergence.reshape(levels * rows, cols),
                cloud.reshape(levels * rows, cols),
                edge_weight,
                inv_area,
                span_of,
            )
        ],
        damping,
        exner,
        sat_scale,
        layer_mass,
    )
    shape = (levels, rows, cols)
    theta_next, vapor_next, cloud_next, divergence_next, precip = pl.pallas_call(
        placing,
        out_shape=tuple(jax.ShapeDtypeStruct(array.shape, array.dtype) for array in made),
        in_specs=[anywhere] * 5,
        out_specs=(far,) * 5,
        scratch_shapes=[pltpu.SemaphoreType.DMA((len(made), 2))],
    )(*made)
    return (
        theta_next.reshape(shape),
        vapor_next.reshape(shape),
        cloud_next.reshape(shape),
        divergence_next.reshape(shape),
        precip.reshape(1, block * LANES),
    )


def solution(mesh):
    placed = (
        P(None, "px", "py"),
        P(None, "px", "py"),
        P(None, "px", "py"),
        P(None, "px", "py"),
        P(None, "px", "py"),
        P("px", "py"),
        P(),
        P(),
        P(),
        P(),
        P("px", "py"),
    )
    return jax.shard_map(
        functools.partial(on_device, mesh.shape["px"], mesh.shape["py"]),
        mesh=mesh,
        in_specs=placed,
        out_specs=(
            P(None, "px", "py"),
            P(None, "px", "py"),
            P(None, "px", "py"),
            P(None, "px", "py"),
            P("px", "py"),
        ),
        check_vma=False,
    )
```

```python
import functools

import jax
import jax.numpy as jnp
from jax import lax
from jax.experimental import pallas as pl
from jax.experimental.pallas import tpu as pltpu
from jax.sharding import PartitionSpec as P

NSAT = 2
LATENT = 0.5
QCRIT = 0.2
AUTO_RATE = 0.5

MESH = pl.DeviceIdType.MESH
LANES = 128
SUB = 8
CORNERS = ((1, 1), (1, -1), (-1, 1), (-1, -1))


def kernel(
    dims,
    theta,
    vapor,
    divergence,
    cloud,
    edge_weight,
    inv_area,
    span_of,
    damping,
    exner,
    sat_scale,
    layer_mass,
    theta_out,
    vapor_out,
    cloud_out,
    divergence_out,
    precip_out,
    nat,
    out,
    grid,
    lap,
    coef,
    consts,
    weights,
    areas,
    spans,
    col_send,
    col_recv,
    corner_send,
    corner_recv,
    high,
    low,
    rain_rows,
    rain_send,
    rain_recv,
    in_sem,
    out_sem,
    send_sem,
    recv_sem,
    rain_send_sem,
    rain_recv_sem,
):
    n_px, n_py, levels, rows, cols = dims
    pad = consts.shape[1]
    halves = cols // LANES
    groups = 3 * pad // SUB
    wide = cols + LANES
    block = rows * cols // LANES
    px = lax.axis_index("px")
    py = lax.axis_index("py")
    used = levels * rows

    def device(dx, dy):
        return (lax.rem(px + dx + n_px, n_px), lax.rem(py + dy + n_py, n_py))

    loads = []
    for source, target in ((span_of, spans), (edge_weight, weights), (inv_area, areas)):
        loads.append(pltpu.make_async_copy(source, target, in_sem.at[len(loads)]))
    for f, source in enumerate((theta, vapor, divergence, cloud)):
        for h in range(halves):
            loads.append(
                pltpu.make_async_copy(
                    source.at[:, pl.ds(h * LANES, LANES)],
                    nat.at[f, h, pl.ds(0, used), :],
                    in_sem.at[len(loads)],
                )
            )
    for load in loads:
        load.start()

    barrier = pltpu.get_barrier_semaphore()
    greeted = [(1, 0), (-1, 0)] + list(CORNERS) + [(0, d) for d in range(1, n_py)]
    for dx, dy in greeted:
        pl.semaphore_signal(barrier, inc=1, device_id=device(dx, dy), device_id_type=MESH)

    def fill(level, carry):
        at = pl.ds(level, 1)
        for k in range(3):
            consts[k, at, :] = jnp.full((1, LANES), damping[k, level], jnp.float32)
        consts[3, at, :] = jnp.full((1, LANES), exner[level], jnp.float32)
        consts[4, at, :] = jnp.full((1, LANES), sat_scale[level], jnp.float32)
        consts[5, at, :] = jnp.full((1, LANES), layer_mass[level], jnp.float32)
        return carry

    for k in range(6):
        start = levels // SUB * SUB
        consts[k, pl.ds(start, pad - start), :] = jnp.full(
            (pad - start, LANES), 1.0 if k == 3 else 0.0, jnp.float32
        )
    lax.fori_loop(0, levels, fill, 0)
    consts[6] = LATENT / consts[3]
    for f in range(4):
        for h in range(halves):
            nat[f, h, pl.ds(used, (pad - levels) * rows), :] = jnp.zeros(
                ((pad - levels) * rows, LANES), jnp.float32
            )

    loads[0].wait()
    high_count = high.shape[0]

    def upper(i, carry):
        place = spans[pl.ds(i, 1), :] // LANES
        rank = lax.broadcasted_iota(jnp.int32, (high_count, cols), 0)
        hit = jnp.where(rank == place, 1.0, 0.0).astype(jnp.bfloat16)
        high[:, pl.ds(pl.multiple_of(i * cols, cols), cols)] = hit
        return carry

    lax.fori_loop(0, rows, upper, 0)

    for load in loads[1 : 3 + 3 * halves]:
        load.wait()

    def turn(i):
        for f in range(3):
            for h in range(halves):
                grid[i + 2, pl.ds(f * pad, pad), pl.ds(h * LANES, LANES)] = nat[
                    f, h, pl.ds(i, pad, stride=rows), :
                ]
        for k in range(3):
            grid[i + 2, pl.ds(levels + k, 1), pl.ds(0, cols)] = weights[k, pl.ds(i, 1), :]
        grid[i + 2, pl.ds(levels + 3, 1), pl.ds(0, cols)] = areas[pl.ds(i, 1), :]

    def turn_edge(n, carry):
        turn(n + n // 2 * (rows - 4))
        return carry

    lax.fori_loop(0, 4, turn_edge, 0)
    pl.semaphore_wait(barrier, len(greeted))

    sends = []

    def send(source, target, to):
        k = len(sends)
        copy = pltpu.make_async_remote_copy(
            src_ref=source,
            dst_ref=target,
            send_sem=send_sem.at[k],
            recv_sem=recv_sem.at[k],
            device_id=to,
            device_id_type=MESH,
        )
        copy.start()
        sends.append(copy)

    def send_rows(first, count):
        part = pl.ds(first, count)
        lanes = pl.ds(0, cols)
        send(grid.at[pl.ds(rows, 2), part, lanes], grid.at[pl.ds(0, 2), part, lanes], device(1, 0))
        send(
            grid.at[pl.ds(2, 2), part, lanes],
            grid.at[pl.ds(rows + 2, 2), part, lanes],
            device(-1, 0),
        )

    send_rows(0, 2 * pad)

    def turn_inner(n, carry):
        turn(n + 2)
        return carry

    lax.fori_loop(0, rows - 4, turn_inner, 0)

    lane = lax.broadcasted_iota(jnp.int32, (SUB, LANES), 1)
    per = LANES // (2 * rows)

    def edge_tile(r, g, dy):
        first = cols - LANES if dy > 0 else 0
        at = g * SUB if isinstance(g, int) else pl.multiple_of(g * SUB, SUB)
        return grid[r, pl.ds(at, SUB), pl.ds(first, LANES)]

    def pack(q, carry):
        for side, dy in enumerate((1, -1)):
            packed = jnp.zeros((SUB, LANES), jnp.float32)
            for part in range(per):
                for i in range(rows):
                    p = (part * rows + i) * 2
                    shift = (p - (LANES - 2 if dy > 0 else 0)) % LANES
                    moved = edge_tile(i + 2, q * per + part, dy)
                    if shift:
                        moved = pltpu.roll(moved, shift, 1)
                    packed = jnp.where(lane // 2 == p // 2, moved, packed)
            col_send[side, pl.ds(pl.multiple_of(q * SUB, SUB), SUB), :] = packed
        return carry

    lax.fori_loop(0, groups // per, pack, 0)
    send(col_send.at[0], col_recv.at[0], device(0, 1))
    send(col_send.at[1], col_recv.at[1], device(0, -1))

    pair = lane // 2
    for n, (dx, dy) in enumerate(CORNERS):
        packed = jnp.zeros((SUB, LANES), jnp.float32)
        for g in range(groups):
            for k in range(2):
                p = 4 * g + 2 * k
                moved = edge_tile((rows if dx > 0 else 2) + k, g, dy)
                shift = (p + (2 if dy > 0 else 0)) % LANES
                if shift:
                    moved = pltpu.roll(moved, shift, 1)
                packed = jnp.where(pair == p // 2, moved, packed)
        corner_send[n] = packed
        send(corner_send.at[n], corner_recv.at[n], device(dx, dy))
    send_rows(2 * pad, pad)

    sends[2].wait_recv()
    sends[3].wait_recv()

    def unpack(q, carry):
        at = pl.ds(pl.multiple_of(q * SUB, SUB), SUB)
        from_left = col_recv[0, at, :]
        from_right = col_recv[1, at, :]
        for part in range(per):
            for i in range(rows):
                p = (part * rows + i) * 2
                left = pltpu.roll(from_left, (LANES - 2 - p) % LANES, 1) if p != LANES - 2 else from_left
                right = pltpu.roll(from_right, (LANES - p) % LANES, 1) if p else from_right
                g = q * per + part
                grid[i + 2, pl.ds(pl.multiple_of(g * SUB, SUB), SUB), pl.ds(cols, LANES)] = jnp.where(
                    lane < 64, right, left
                )
        return carry

    lax.fori_loop(0, groups // per, unpack, 0)

    def laplace_at(source, r, at, c):
        up = source[r + 1, at, :]
        mid = source[r, at, :]
        down = source[r - 1, at, :]
        from_right = c[3] * mid + c[4] * down
        from_left = c[5] * mid + c[6] * up
        return (
            (c[0] * up + c[1] * down)
            + c[2] * mid
            + pltpu.roll(from_right, wide - 1, 1)
            + pltpu.roll(from_left, 1, 1)
        )

    def geometry(r, k):
        return jnp.broadcast_to(grid[r, pl.ds(levels + k, 1), :], (SUB, wide))

    def first_laplace(r):
        area = geometry(r, 3)
        area_right = pltpu.roll(area, wide - 1, 1)
        ahead = area * geometry(r, 0)
        behind = area * geometry(r - 1, 0)
        to_right = area * geometry(r, 1)
        to_right_behind = area * geometry(r, 2)
        own = geometry(r, 1)
        ahead_own = geometry(r + 1, 2)
        to_left = area_right * own
        to_left_ahead = area_right * ahead_own
        centre = -(
            ahead
            + behind
            + to_right
            + to_right_behind
            + pltpu.roll(to_left, 1, 1)
            + pltpu.roll(to_left_ahead, 1, 1)
        )
        c = (
            ahead,
            behind,
            centre,
            pltpu.roll(to_right, 1, 1),
            pltpu.roll(to_right_behind, 1, 1),
            to_left,
            to_left_ahead,
        )
        for k in range(7):
            coef[r, k] = c[k]

        for g in range(2 * pad // SUB):
            at = pl.ds(g * SUB, SUB)
            lap[r, at, :] = laplace_at(grid, r, at, c)

    def coefficients(r):
        return tuple(coef[r, k] for k in range(7))

    def spread(k, at):
        tile = consts[k, at, :]
        return jnp.concatenate([tile] * halves, axis=1)

    def damped(f, r, q, c):
        at = pl.ds(f * pad + q * SUB, SUB)
        del4 = laplace_at(lap, r, at, c)[:, :cols]
        here = pl.ds(q * SUB, SUB)
        return grid[r, at, pl.ds(0, cols)] - spread(f, here) * del4

    def put(k, r, q, value):
        for h in range(halves):
            out[k, h, pl.ds(q * (SUB * rows) + r - 2, SUB, stride=rows), :] = value[
                :, h * LANES : (h + 1) * LANES
            ]

    def physics(r):
        c = coefficients(r)

        rain = jnp.zeros((SUB, cols), jnp.float32)
        for q in range(pad // SUB):
            here = pl.ds(q * SUB, SUB)
            theta_dyn = damped(0, r, q, c)
            vapor_dyn = damped(1, r, q, c)
            cloud_now = jnp.concatenate(
                [
                    nat[3, h, pl.ds(q * (SUB * rows) + r - 2, SUB, stride=rows), :]
                    for h in range(halves)
                ],
                axis=1,
            )
            temper = theta_dyn * spread(3, here)
            scale = spread(4, here)
            condensed = jnp.zeros_like(temper)
            for repeat in range(NSAT):
                warmed = temper + LATENT * condensed if repeat else temper
                saturation = scale * jnp.exp(warmed)
                excess = vapor_dyn - condensed - saturation
                slope = 1.0 + LATENT * saturation
                inverse = pl.reciprocal(slope, approx=True)
                inverse = inverse * (2.0 - slope * inverse)
                condensed = condensed + excess * inverse
            condensed = jnp.maximum(condensed, -cloud_now)
            put(0, r, q, theta_dyn + condensed * spread(6, here))
            put(1, r, q, vapor_dyn - condensed)
            liquid = cloud_now + condensed
            rained = AUTO_RATE * jnp.maximum(liquid - QCRIT, 0.0)
            put(2, r, q, liquid - rained)
            rain = rain + spread(5, here) * rained
        rain_rows[r - 2] = rain

    rank_low = lax.broadcasted_iota(jnp.int32, (LANES, cols), 0)

    def lower(i):
        total = jnp.sum(rain_rows[i], axis=0, keepdims=True)
        place = lax.rem(spans[pl.ds(i, 1), :], LANES)
        head = total.astype(jnp.bfloat16).astype(jnp.float32)
        at = pl.ds(pl.multiple_of(i * cols, cols), cols)
        hit = rank_low == place
        for k, piece in enumerate((head, total - head)):
            low[pl.ds(k * LANES, LANES), at] = jnp.where(hit, piece, 0.0).astype(jnp.bfloat16)

    def product(first, count):
        at = pl.ds(first * cols, count * cols)
        both = lax.dot_general(
            high[:, at], low[:, at], (((1,), (1,)), ((), ())), preferred_element_type=jnp.float32
        )
        return both[:, :LANES] + both[:, LANES:]

    def loop(first, end, do):
        def step(r, carry):
            do(r)
            return carry

        lax.fori_loop(first, end, step, 0)

    loop(3, rows + 1, first_laplace)
    for h in range(halves):
        loads[3 + 3 * halves + h].wait()
    loop(4, rows, physics)

    def lower_four(n):
        for k in range(4):
            lower(2 + 4 * n + k)

    loop(0, (rows - 4) // 4, lower_four)
    rain_send[...] = product(2, rows - 4)

    for k in (0, 1, 4, 5, 6, 7):
        sends[k].wait_recv()

    for dx in (1, -1):
        for g in range(groups):
            for k in range(2):
                p = 4 * g + 2 * k
                left = corner_recv[CORNERS.index((dx, 1))]
                right = corner_recv[CORNERS.index((dx, -1))]
                left = pltpu.roll(left, (LANES - 2 - p) % LANES, 1) if p != LANES - 2 else left
                right = pltpu.roll(right, LANES - p, 1) if p else right
                r = k if dx > 0 else rows + 2 + k
                grid[r, pl.ds(g * SUB, SUB), pl.ds(cols, LANES)] = jnp.where(lane < 64, right, left)
    loop(0, 4, lambda n: first_laplace(n + 1 + n // 2 * (rows - 2)))
    loop(0, 4, lambda n: physics(n + 2 + n // 2 * (rows - 4)))

    for i in (0, 1, rows - 2, rows - 1):
        lower(i)

    rain_send[...] += product(0, 2) + product(rows - 2, 2)
    rains = []
    for d in range(1, n_py):
        to = device(0, d)
        copy = pltpu.make_async_remote_copy(
            src_ref=rain_send.at[pl.ds(pl.multiple_of(to[1] * block, block), block), :],
            dst_ref=rain_recv.at[d - 1],
            send_sem=rain_send_sem.at[d - 1],
            recv_sem=rain_recv_sem.at[d - 1],
            device_id=to,
            device_id_type=MESH,
        )
        copy.start()
        rains.append(copy)

    stores = []

    def store(k, target):
        for h in range(halves):
            copy = pltpu.make_async_copy(
                out.at[k, h, pl.ds(0, used), :],
                target.at[:, pl.ds(h * LANES, LANES)],
                out_sem.at[len(stores)],
            )
            copy.start()
            stores.append(copy)

    store(0, theta_out)
    store(1, vapor_out)
    store(2, cloud_out)

    for k in (8, 9):
        sends[k].wait_recv()

    def diverge_first(n):
        for r in (1 + 2 * n, 2 + 2 * n):
            c = coefficients(r)
            for g in range(2 * pad // SUB, groups):
                at = pl.ds(g * SUB, SUB)
                lap[r, at, :] = laplace_at(grid, r, at, c)

    def diverge(n):
        for r in (2 + 2 * n, 3 + 2 * n):
            c = coefficients(r)
            for q in range(pad // SUB):
                put(3, r, q, damped(2, r, q, c))

    loop(0, rows // 2 + 1, diverge_first)
    loop(0, rows // 2, diverge)
    store(3, divergence_out)

    total = rain_send[pl.ds(pl.multiple_of(py * block, block), block), :]
    for d in range(1, n_py):
        rains[d - 1].wait_recv()
        total = total + rain_recv[d - 1]
    precip_out[...] = total
    for copy in sends:
        copy.wait_send()
    for copy in rains:
        copy.wait_send()
    for copy in stores:
        copy.wait()


def placing(*refs):
    count = len(refs) // 2
    sem = refs[-1]
    copies = []
    for k in range(count):
        half = refs[k].shape[0] // 2
        for part in range(2):
            at = pl.ds(part * half, half)
            copies.append(
                pltpu.make_async_copy(refs[k].at[at], refs[count + k].at[at], sem.at[k, part])
            )
    for copy in copies:
        copy.start()
    for copy in copies:
        copy.wait()


def on_device(
    n_px,
    n_py,
    theta,
    vapor,
    cloud,
    divergence,
    edge_weight,
    inv_area,
    damping,
    exner,
    sat_scale,
    layer_mass,
    span_of,
):
    levels, rows, cols = theta.shape
    pad = (levels + 4 + SUB - 1) // SUB * SUB
    halves = cols // LANES
    wide = cols + LANES
    block = rows * cols // LANES
    flat = jax.ShapeDtypeStruct((levels * rows, cols), jnp.float32)
    f32 = jnp.float32
    anywhere = pl.BlockSpec(memory_space=pl.ANY)
    far = pl.BlockSpec(memory_space=pltpu.HBM)
    scalars = pl.BlockSpec(memory_space=pltpu.SMEM)
    made = pl.pallas_call(
        functools.partial(kernel, (n_px, n_py, levels, rows, cols)),
        out_shape=(flat, flat, flat, flat, jax.ShapeDtypeStruct((block, LANES), f32)),
        in_specs=[far] * 7 + [scalars] * 4,
        out_specs=(anywhere,) * 4 + (pl.BlockSpec(memory_space=pltpu.VMEM),),
        scratch_shapes=[
            pltpu.VMEM((4, halves, pad * rows, LANES), f32),
            pltpu.VMEM((4, halves, pad * rows, LANES), f32),
            pltpu.VMEM((rows + 4, 3 * pad, wide), f32),
            pltpu.VMEM((rows + 4, 3 * pad, wide), f32),
            pltpu.VMEM((rows + 4, 7, SUB, wide), f32),
            pltpu.VMEM((7, pad, LANES), f32),
            pltpu.VMEM((3, rows, cols), f32),
            pltpu.VMEM((rows, cols), f32),
            pltpu.VMEM((rows, cols), jnp.int32),
            pltpu.VMEM((2, 3 * pad * 2 * rows // LANES, LANES), f32),
            pltpu.VMEM((2, 3 * pad * 2 * rows // LANES, LANES), f32),
            pltpu.VMEM((4, SUB, LANES), f32),
            pltpu.VMEM((4, SUB, LANES), f32),
            pltpu.VMEM((n_py * block, rows * cols), jnp.bfloat16),
            pltpu.VMEM((2 * LANES, rows * cols), jnp.bfloat16),
            pltpu.VMEM((rows, SUB, cols), f32),
            pltpu.VMEM((n_py * block, LANES), f32),
            pltpu.VMEM((n_py - 1, block, LANES), f32),
            pltpu.SemaphoreType.DMA((4 * halves + 3,)),
            pltpu.SemaphoreType.DMA((4 * halves,)),
            pltpu.SemaphoreType.DMA((10,)),
            pltpu.SemaphoreType.DMA((10,)),
            pltpu.SemaphoreType.DMA((n_py - 1,)),
            pltpu.SemaphoreType.DMA((n_py - 1,)),
        ],
        compiler_params=pltpu.CompilerParams(
            collective_id=0, has_side_effects=True, vmem_limit_bytes=40 * 1024 * 1024
        ),
        cost_estimate=pl.CostEstimate(
            flops=60 * levels * rows * cols, bytes_accessed=32 * levels * rows * cols, transcendentals=0
        ),
    )(
        *[
            pltpu.with_memory_space_constraint(array, pltpu.HBM)
            for array in (
                theta.reshape(levels * rows, cols),
                vapor.reshape(levels * rows, cols),
                divergence.reshape(levels * rows, cols),
                cloud.reshape(levels * rows, cols),
                edge_weight,
                inv_area,
                span_of,
            )
        ],
        damping,
        exner,
        sat_scale,
        layer_mass,
    )
    shape = (levels, rows, cols)
    theta_next, vapor_next, cloud_next, divergence_next, precip = pl.pallas_call(
        placing,
        out_shape=tuple(jax.ShapeDtypeStruct(array.shape, array.dtype) for array in made),
        in_specs=[pl.BlockSpec(memory_space=pltpu.VMEM)] * 5,
        out_specs=(far,) * 5,
        scratch_shapes=[pltpu.SemaphoreType.DMA((len(made), 2))],
        compiler_params=pltpu.CompilerParams(vmem_limit_bytes=1024 * 1024),
    )(*[pltpu.with_memory_space_constraint(array, pltpu.VMEM) for array in made])
    return (
        theta_next.reshape(shape),
        vapor_next.reshape(shape),
        cloud_next.reshape(shape),
        divergence_next.reshape(shape),
        precip.reshape(1, block * LANES),
    )


def solution(mesh):
    placed = (
        P(None, "px", "py"),
        P(None, "px", "py"),
        P(None, "px", "py"),
        P(None, "px", "py"),
        P(None, "px", "py"),
        P("px", "py"),
        P(),
        P(),
        P(),
        P(),
        P("px", "py"),
    )
    return jax.shard_map(
        functools.partial(on_device, mesh.shape["px"], mesh.shape["py"]),
        mesh=mesh,
        in_specs=placed,
        out_specs=(
            P(None, "px", "py"),
            P(None, "px", "py"),
            P(None, "px", "py"),
            P(None, "px", "py"),
            P("px", "py"),
        ),
        check_vma=False,
    )
```

```python
import functools

import jax
import jax.numpy as jnp
from jax import lax
from jax.experimental import pallas as pl
from jax.experimental.pallas import tpu as pltpu
from jax.sharding import PartitionSpec as P

NSAT = 2
LATENT = 0.5
QCRIT = 0.2
AUTO_RATE = 0.5

MESH = pl.DeviceIdType.MESH
LANES = 128
SUB = 8
CORNERS = ((1, 1), (1, -1), (-1, 1), (-1, -1))


def kernel(
    dims,
    theta,
    vapor,
    divergence,
    cloud,
    edge_weight,
    inv_area,
    span_of,
    damping,
    exner,
    sat_scale,
    layer_mass,
    theta_out,
    vapor_out,
    cloud_out,
    divergence_out,
    precip_out,
    nat,
    out,
    made,
    grid,
    lap,
    coef,
    consts,
    weights,
    areas,
    spans,
    col_send,
    col_recv,
    corner_send,
    corner_recv,
    high,
    low,
    rain_rows,
    rain_send,
    rain_recv,
    in_sem,
    out_sem,
    send_sem,
    recv_sem,
    rain_send_sem,
    rain_recv_sem,
):
    n_px, n_py, levels, rows, cols = dims
    pad = consts.shape[1]
    halves = cols // LANES
    groups = 3 * pad // SUB
    wide = cols + LANES
    block = rows * cols // LANES
    px = lax.axis_index("px")
    py = lax.axis_index("py")
    used = levels * rows

    def device(dx, dy):
        return (lax.rem(px + dx + n_px, n_px), lax.rem(py + dy + n_py, n_py))

    loads = []
    for source, target in ((span_of, spans), (edge_weight, weights), (inv_area, areas)):
        loads.append(pltpu.make_async_copy(source, target, in_sem.at[len(loads)]))
    for f, source in enumerate((theta, vapor, divergence, cloud)):
        for h in range(halves):
            loads.append(
                pltpu.make_async_copy(
                    source.at[:, pl.ds(h * LANES, LANES)],
                    nat.at[f, h, pl.ds(0, used), :],
                    in_sem.at[len(loads)],
                )
            )
    for load in loads:
        load.start()

    barrier = pltpu.get_barrier_semaphore()
    greeted = [(1, 0), (-1, 0)] + list(CORNERS) + [(0, d) for d in range(1, n_py)]
    for dx, dy in greeted:
        pl.semaphore_signal(barrier, inc=1, device_id=device(dx, dy), device_id_type=MESH)

    def fill(level, carry):
        at = pl.ds(level, 1)
        for k in range(3):
            consts[k, at, :] = jnp.full((1, LANES), damping[k, level], jnp.float32)
        consts[3, at, :] = jnp.full((1, LANES), exner[level], jnp.float32)
        consts[4, at, :] = jnp.full((1, LANES), sat_scale[level], jnp.float32)
        consts[5, at, :] = jnp.full((1, LANES), layer_mass[level], jnp.float32)
        return carry

    for k in range(6):
        start = levels // SUB * SUB
        consts[k, pl.ds(start, pad - start), :] = jnp.full(
            (pad - start, LANES), 1.0 if k == 3 else 0.0, jnp.float32
        )
    lax.fori_loop(0, levels, fill, 0)
    consts[6] = LATENT / consts[3]
    for f in range(4):
        for h in range(halves):
            nat[f, h, pl.ds(used, (pad - levels) * rows), :] = jnp.zeros(
                ((pad - levels) * rows, LANES), jnp.float32
            )

    loads[0].wait()
    high_count = high.shape[0]

    def upper(i, carry):
        place = spans[pl.ds(i, 1), :] // LANES
        rank = lax.broadcasted_iota(jnp.int32, (high_count, cols), 0)
        hit = jnp.where(rank == place, 1.0, 0.0).astype(jnp.bfloat16)
        high[:, pl.ds(pl.multiple_of(i * cols, cols), cols)] = hit
        return carry

    lax.fori_loop(0, rows, upper, 0)

    for load in loads[1 : 3 + 3 * halves]:
        load.wait()

    def turned(f, q, h):
        block_rows = nat[f, h, pl.ds(pl.multiple_of(q * (SUB * rows), SUB * rows), SUB * rows), :]
        return jnp.swapaxes(block_rows.reshape(SUB, rows, LANES), 0, 1)

    def turn(q, carry):
        for f in range(3):
            for h in range(halves):
                at = pl.ds(pl.multiple_of(f * pad + q * SUB, SUB), SUB)
                grid[pl.ds(2, rows), at, pl.ds(h * LANES, LANES)] = turned(f, q, h)
        return carry

    lax.fori_loop(0, pad // SUB, turn, 0)

    def turn_geometry(i, carry):
        for k in range(3):
            grid[i + 2, pl.ds(levels + k, 1), pl.ds(0, cols)] = weights[k, pl.ds(i, 1), :]
        grid[i + 2, pl.ds(levels + 3, 1), pl.ds(0, cols)] = areas[pl.ds(i, 1), :]
        return carry

    lax.fori_loop(0, rows, turn_geometry, 0)
    pl.semaphore_wait(barrier, len(greeted))

    sends = []

    def send(source, target, to):
        k = len(sends)
        copy = pltpu.make_async_remote_copy(
            src_ref=source,
            dst_ref=target,
            send_sem=send_sem.at[k],
            recv_sem=recv_sem.at[k],
            device_id=to,
            device_id_type=MESH,
        )
        copy.start()
        sends.append(copy)

    def send_rows(first, count):
        part = pl.ds(first, count)
        lanes = pl.ds(0, cols)
        send(grid.at[pl.ds(rows, 2), part, lanes], grid.at[pl.ds(0, 2), part, lanes], device(1, 0))
        send(
            grid.at[pl.ds(2, 2), part, lanes],
            grid.at[pl.ds(rows + 2, 2), part, lanes],
            device(-1, 0),
        )

    send_rows(0, 2 * pad)

    lane = lax.broadcasted_iota(jnp.int32, (SUB, LANES), 1)
    per = LANES // (2 * rows)

    def edge_tile(r, g, dy):
        first = cols - LANES if dy > 0 else 0
        at = g * SUB if isinstance(g, int) else pl.multiple_of(g * SUB, SUB)
        return grid[r, pl.ds(at, SUB), pl.ds(first, LANES)]

    def pack(q, carry):
        for side, dy in enumerate((1, -1)):
            packed = jnp.zeros((SUB, LANES), jnp.float32)
            for part in range(per):
                for i in range(rows):
                    p = (part * rows + i) * 2
                    shift = (p - (LANES - 2 if dy > 0 else 0)) % LANES
                    moved = edge_tile(i + 2, q * per + part, dy)
                    if shift:
                        moved = pltpu.roll(moved, shift, 1)
                    packed = jnp.where(lane // 2 == p // 2, moved, packed)
            col_send[side, pl.ds(pl.multiple_of(q * SUB, SUB), SUB), :] = packed
        return carry

    lax.fori_loop(0, groups // per, pack, 0)
    send(col_send.at[0], col_recv.at[0], device(0, 1))
    send(col_send.at[1], col_recv.at[1], device(0, -1))

    pair = lane // 2
    for n, (dx, dy) in enumerate(CORNERS):
        packed = jnp.zeros((SUB, LANES), jnp.float32)
        for g in range(groups):
            for k in range(2):
                p = 4 * g + 2 * k
                moved = edge_tile((rows if dx > 0 else 2) + k, g, dy)
                shift = (p + (2 if dy > 0 else 0)) % LANES
                if shift:
                    moved = pltpu.roll(moved, shift, 1)
                packed = jnp.where(pair == p // 2, moved, packed)
        corner_send[n] = packed
        send(corner_send.at[n], corner_recv.at[n], device(dx, dy))
    send_rows(2 * pad, pad)

    sends[2].wait_recv()
    sends[3].wait_recv()

    def unpack(q, carry):
        at = pl.ds(pl.multiple_of(q * SUB, SUB), SUB)
        from_left = col_recv[0, at, :]
        from_right = col_recv[1, at, :]
        for part in range(per):
            for i in range(rows):
                p = (part * rows + i) * 2
                left = pltpu.roll(from_left, (LANES - 2 - p) % LANES, 1) if p != LANES - 2 else from_left
                right = pltpu.roll(from_right, (LANES - p) % LANES, 1) if p else from_right
                g = q * per + part
                grid[i + 2, pl.ds(pl.multiple_of(g * SUB, SUB), SUB), pl.ds(cols, LANES)] = jnp.where(
                    lane < 64, right, left
                )
        return carry

    lax.fori_loop(0, groups // per, unpack, 0)

    def laplace_at(source, r, at, c):
        up = source[r + 1, at, :]
        mid = source[r, at, :]
        down = source[r - 1, at, :]
        from_right = c[3] * mid + c[4] * down
        from_left = c[5] * mid + c[6] * up
        return (
            (c[0] * up + c[1] * down)
            + c[2] * mid
            + pltpu.roll(from_right, wide - 1, 1)
            + pltpu.roll(from_left, 1, 1)
        )

    def geometry(r, k):
        return jnp.broadcast_to(grid[r, pl.ds(levels + k, 1), :], (SUB, wide))

    def first_laplace(r):
        area = geometry(r, 3)
        area_right = pltpu.roll(area, wide - 1, 1)
        ahead = area * geometry(r, 0)
        behind = area * geometry(r - 1, 0)
        to_right = area * geometry(r, 1)
        to_right_behind = area * geometry(r, 2)
        own = geometry(r, 1)
        ahead_own = geometry(r + 1, 2)
        to_left = area_right * own
        to_left_ahead = area_right * ahead_own
        centre = -(
            ahead
            + behind
            + to_right
            + to_right_behind
            + pltpu.roll(to_left, 1, 1)
            + pltpu.roll(to_left_ahead, 1, 1)
        )
        c = (
            ahead,
            behind,
            centre,
            pltpu.roll(to_right, 1, 1),
            pltpu.roll(to_right_behind, 1, 1),
            to_left,
            to_left_ahead,
        )
        for k in range(7):
            coef[r, k] = c[k]

        for g in range(2 * pad // SUB):
            at = pl.ds(g * SUB, SUB)
            lap[r, at, :] = laplace_at(grid, r, at, c)

    def coefficients(r):
        return tuple(coef[r, k] for k in range(7))

    def spread(k, at):
        tile = consts[k, at, :]
        return jnp.concatenate([tile] * halves, axis=1)

    def damped(f, r, q, c):
        at = pl.ds(f * pad + q * SUB, SUB)
        del4 = laplace_at(lap, r, at, c)[:, :cols]
        here = pl.ds(q * SUB, SUB)
        return grid[r, at, pl.ds(0, cols)] - spread(f, here) * del4

    def put(k, r, q, value):
        made[k, r - 2, pl.ds(q * SUB, SUB), :] = value

    def physics(r):
        c = coefficients(r)

        rain = jnp.zeros((SUB, cols), jnp.float32)
        for q in range(pad // SUB):
            here = pl.ds(q * SUB, SUB)
            theta_dyn = damped(0, r, q, c)
            vapor_dyn = damped(1, r, q, c)
            cloud_now = made[2, r - 2, here, :]
            temper = theta_dyn * spread(3, here)
            scale = spread(4, here)
            condensed = jnp.zeros_like(temper)
            for repeat in range(NSAT):
                warmed = temper + LATENT * condensed if repeat else temper
                saturation = scale * jnp.exp(warmed)
                excess = vapor_dyn - condensed - saturation
                slope = 1.0 + LATENT * saturation
                inverse = pl.reciprocal(slope, approx=True)
                inverse = inverse * (2.0 - slope * inverse)
                condensed = condensed + excess * inverse
            condensed = jnp.maximum(condensed, -cloud_now)
            put(0, r, q, theta_dyn + condensed * spread(6, here))
            put(1, r, q, vapor_dyn - condensed)
            liquid = cloud_now + condensed
            rained = AUTO_RATE * jnp.maximum(liquid - QCRIT, 0.0)
            put(2, r, q, liquid - rained)
            rain = rain + spread(5, here) * rained
        rain_rows[r - 2] = rain

    rank_low = lax.broadcasted_iota(jnp.int32, (LANES, cols), 0)

    def lower(i):
        total = jnp.sum(rain_rows[i], axis=0, keepdims=True)
        place = lax.rem(spans[pl.ds(i, 1), :], LANES)
        head = total.astype(jnp.bfloat16).astype(jnp.float32)
        at = pl.ds(pl.multiple_of(i * cols, cols), cols)
        hit = rank_low == place
        for k, piece in enumerate((head, total - head)):
            low[pl.ds(k * LANES, LANES), at] = jnp.where(hit, piece, 0.0).astype(jnp.bfloat16)

    def product(first, count):
        at = pl.ds(first * cols, count * cols)
        both = lax.dot_general(
            high[:, at], low[:, at], (((1,), (1,)), ((), ())), preferred_element_type=jnp.float32
        )
        return both[:, :LANES] + both[:, LANES:]

    def loop(first, end, do):
        def step(r, carry):
            do(r)
            return carry

        lax.fori_loop(first, end, step, 0)

    loop(3, rows + 1, first_laplace)
    for h in range(halves):
        loads[3 + 3 * halves + h].wait()

    def turn_cloud(q, carry):
        for h in range(halves):
            at = pl.ds(pl.multiple_of(q * SUB, SUB), SUB)
            made[2, :, at, pl.ds(h * LANES, LANES)] = turned(3, q, h)
        return carry

    lax.fori_loop(0, pad // SUB, turn_cloud, 0)
    loop(4, rows, physics)

    def lower_four(n):
        for k in range(4):
            lower(2 + 4 * n + k)

    loop(0, (rows - 4) // 4, lower_four)
    rain_send[...] = product(2, rows - 4)

    for k in (0, 1, 4, 5, 6, 7):
        sends[k].wait_recv()

    for dx in (1, -1):
        for g in range(groups):
            for k in range(2):
                p = 4 * g + 2 * k
                left = corner_recv[CORNERS.index((dx, 1))]
                right = corner_recv[CORNERS.index((dx, -1))]
                left = pltpu.roll(left, (LANES - 2 - p) % LANES, 1) if p != LANES - 2 else left
                right = pltpu.roll(right, LANES - p, 1) if p else right
                r = k if dx > 0 else rows + 2 + k
                grid[r, pl.ds(g * SUB, SUB), pl.ds(cols, LANES)] = jnp.where(lane < 64, right, left)
    loop(0, 4, lambda n: first_laplace(n + 1 + n // 2 * (rows - 2)))
    loop(0, 4, lambda n: physics(n + 2 + n // 2 * (rows - 4)))

    for i in (0, 1, rows - 2, rows - 1):
        lower(i)

    rain_send[...] += product(0, 2) + product(rows - 2, 2)
    rains = []
    for d in range(1, n_py):
        to = device(0, d)
        copy = pltpu.make_async_remote_copy(
            src_ref=rain_send.at[pl.ds(pl.multiple_of(to[1] * block, block), block), :],
            dst_ref=rain_recv.at[d - 1],
            send_sem=rain_send_sem.at[d - 1],
            recv_sem=rain_recv_sem.at[d - 1],
            device_id=to,
            device_id_type=MESH,
        )
        copy.start()
        rains.append(copy)

    stores = []

    def turn_back(k):
        def step(q, carry):
            for h in range(halves):
                at = pl.ds(pl.multiple_of(q * SUB, SUB), SUB)
                back = jnp.swapaxes(made[k, :, at, pl.ds(h * LANES, LANES)], 0, 1)
                to = pl.ds(pl.multiple_of(q * (SUB * rows), SUB * rows), SUB * rows)
                out[k, h, to, :] = back.reshape(SUB * rows, LANES)
            return carry

        lax.fori_loop(0, pad // SUB, step, 0)

    def store(k, target):
        turn_back(k)
        for h in range(halves):
            copy = pltpu.make_async_copy(
                out.at[k, h, pl.ds(0, used), :],
                target.at[:, pl.ds(h * LANES, LANES)],
                out_sem.at[len(stores)],
            )
            copy.start()
            stores.append(copy)

    store(0, theta_out)
    store(1, vapor_out)
    store(2, cloud_out)

    for k in (8, 9):
        sends[k].wait_recv()

    def diverge_first(n):
        for r in (1 + 2 * n, 2 + 2 * n):
            c = coefficients(r)
            for g in range(2 * pad // SUB, groups):
                at = pl.ds(g * SUB, SUB)
                lap[r, at, :] = laplace_at(grid, r, at, c)

    def diverge(n):
        for r in (2 + 2 * n, 3 + 2 * n):
            c = coefficients(r)
            for q in range(pad // SUB):
                put(3, r, q, damped(2, r, q, c))

    loop(0, rows // 2 + 1, diverge_first)
    loop(0, rows // 2, diverge)
    store(3, divergence_out)

    total = rain_send[pl.ds(pl.multiple_of(py * block, block), block), :]
    for d in range(1, n_py):
        rains[d - 1].wait_recv()
        total = total + rain_recv[d - 1]
    precip_out[...] = total
    for copy in sends:
        copy.wait_send()
    for copy in rains:
        copy.wait_send()
    for copy in stores:
        copy.wait()


def placing(*refs):
    count = len(refs) // 2
    sem = refs[-1]
    copies = []
    for k in range(count):
        half = refs[k].shape[0] // 2
        for part in range(2):
            at = pl.ds(part * half, half)
            copies.append(
                pltpu.make_async_copy(refs[k].at[at], refs[count + k].at[at], sem.at[k, part])
            )
    for copy in copies:
        copy.start()
    for copy in copies:
        copy.wait()


def on_device(
    n_px,
    n_py,
    theta,
    vapor,
    cloud,
    divergence,
    edge_weight,
    inv_area,
    damping,
    exner,
    sat_scale,
    layer_mass,
    span_of,
):
    levels, rows, cols = theta.shape
    pad = (levels + 4 + SUB - 1) // SUB * SUB
    halves = cols // LANES
    wide = cols + LANES
    block = rows * cols // LANES
    flat = jax.ShapeDtypeStruct((levels * rows, cols), jnp.float32)
    f32 = jnp.float32
    anywhere = pl.BlockSpec(memory_space=pl.ANY)
    far = pl.BlockSpec(memory_space=pltpu.HBM)
    scalars = pl.BlockSpec(memory_space=pltpu.SMEM)
    made = pl.pallas_call(
        functools.partial(kernel, (n_px, n_py, levels, rows, cols)),
        out_shape=(flat, flat, flat, flat, jax.ShapeDtypeStruct((block, LANES), f32)),
        in_specs=[far] * 7 + [scalars] * 4,
        out_specs=(anywhere,) * 4 + (pl.BlockSpec(memory_space=pltpu.VMEM),),
        scratch_shapes=[
            pltpu.VMEM((4, halves, pad * rows, LANES), f32),
            pltpu.VMEM((4, halves, pad * rows, LANES), f32),
            pltpu.VMEM((4, rows, pad, cols), f32),
            pltpu.VMEM((rows + 4, 3 * pad, wide), f32),
            pltpu.VMEM((rows + 4, 3 * pad, wide), f32),
            pltpu.VMEM((rows + 4, 7, SUB, wide), f32),
            pltpu.VMEM((7, pad, LANES), f32),
            pltpu.VMEM((3, rows, cols), f32),
            pltpu.VMEM((rows, cols), f32),
            pltpu.VMEM((rows, cols), jnp.int32),
            pltpu.VMEM((2, 3 * pad * 2 * rows // LANES, LANES), f32),
            pltpu.VMEM((2, 3 * pad * 2 * rows // LANES, LANES), f32),
            pltpu.VMEM((4, SUB, LANES), f32),
            pltpu.VMEM((4, SUB, LANES), f32),
            pltpu.VMEM((n_py * block, rows * cols), jnp.bfloat16),
            pltpu.VMEM((2 * LANES, rows * cols), jnp.bfloat16),
            pltpu.VMEM((rows, SUB, cols), f32),
            pltpu.VMEM((n_py * block, LANES), f32),
            pltpu.VMEM((n_py - 1, block, LANES), f32),
            pltpu.SemaphoreType.DMA((4 * halves + 3,)),
            pltpu.SemaphoreType.DMA((4 * halves,)),
            pltpu.SemaphoreType.DMA((10,)),
            pltpu.SemaphoreType.DMA((10,)),
            pltpu.SemaphoreType.DMA((n_py - 1,)),
            pltpu.SemaphoreType.DMA((n_py - 1,)),
        ],
        compiler_params=pltpu.CompilerParams(
            collective_id=0, has_side_effects=True, vmem_limit_bytes=40 * 1024 * 1024
        ),
        cost_estimate=pl.CostEstimate(
            flops=60 * levels * rows * cols, bytes_accessed=32 * levels * rows * cols, transcendentals=0
        ),
    )(
        *[
            pltpu.with_memory_space_constraint(array, pltpu.HBM)
            for array in (
                theta.reshape(levels * rows, cols),
                vapor.reshape(levels * rows, cols),
                divergence.reshape(levels * rows, cols),
                cloud.reshape(levels * rows, cols),
                edge_weight,
                inv_area,
                span_of,
            )
        ],
        damping,
        exner,
        sat_scale,
        layer_mass,
    )
    shape = (levels, rows, cols)
    theta_next, vapor_next, cloud_next, divergence_next, precip = pl.pallas_call(
        placing,
        out_shape=tuple(jax.ShapeDtypeStruct(array.shape, array.dtype) for array in made),
        in_specs=[pl.BlockSpec(memory_space=pltpu.VMEM)] * 5,
        out_specs=(far,) * 5,
        scratch_shapes=[pltpu.SemaphoreType.DMA((len(made), 2))],
        compiler_params=pltpu.CompilerParams(vmem_limit_bytes=1024 * 1024),
    )(*[pltpu.with_memory_space_constraint(array, pltpu.VMEM) for array in made])
    return (
        theta_next.reshape(shape),
        vapor_next.reshape(shape),
        cloud_next.reshape(shape),
        divergence_next.reshape(shape),
        precip.reshape(1, block * LANES),
    )


def solution(mesh):
    placed = (
        P(None, "px", "py"),
        P(None, "px", "py"),
        P(None, "px", "py"),
        P(None, "px", "py"),
        P(None, "px", "py"),
        P("px", "py"),
        P(),
        P(),
        P(),
        P(),
        P("px", "py"),
    )
    return jax.shard_map(
        functools.partial(on_device, mesh.shape["px"], mesh.shape["py"]),
        mesh=mesh,
        in_specs=placed,
        out_specs=(
            P(None, "px", "py"),
            P(None, "px", "py"),
            P(None, "px", "py"),
            P(None, "px", "py"),
            P("px", "py"),
        ),
        check_vma=False,
    )
```

```python
import functools

import jax
import jax.numpy as jnp
from jax import lax
from jax.experimental import pallas as pl
from jax.experimental.pallas import tpu as pltpu
from jax.sharding import PartitionSpec as P

NSAT = 2
LATENT = 0.5
QCRIT = 0.2
AUTO_RATE = 0.5

MESH = pl.DeviceIdType.MESH
LANES = 128
SUB = 8
CORNERS = ((1, 1), (1, -1), (-1, 1), (-1, -1))


def kernel(
    dims,
    theta,
    vapor,
    divergence,
    cloud,
    edge_weight,
    inv_area,
    span_of,
    damping,
    exner,
    sat_scale,
    layer_mass,
    theta_out,
    vapor_out,
    cloud_out,
    divergence_out,
    precip_out,
    nat,
    out,
    made,
    grid,
    lap,
    coef,
    consts,
    weights,
    areas,
    spans,
    col_send,
    col_recv,
    corner_send,
    corner_recv,
    high,
    low,
    rain_rows,
    rain_send,
    rain_recv,
    in_sem,
    out_sem,
    send_sem,
    recv_sem,
    rain_send_sem,
    rain_recv_sem,
):
    n_px, n_py, levels, rows, cols = dims
    pad = consts.shape[1]
    halves = cols // LANES
    groups = 3 * pad // SUB
    wide = cols + LANES
    block = rows * cols // LANES
    px = lax.axis_index("px")
    py = lax.axis_index("py")
    used = levels * rows

    def device(dx, dy):
        return (lax.rem(px + dx + n_px, n_px), lax.rem(py + dy + n_py, n_py))

    loads = []
    for source, target in ((span_of, spans), (edge_weight, weights), (inv_area, areas)):
        loads.append(pltpu.make_async_copy(source, target, in_sem.at[len(loads)]))
    for f, source in enumerate((theta, vapor, divergence, cloud)):
        for h in range(halves):
            loads.append(
                pltpu.make_async_copy(
                    source.at[:, pl.ds(h * LANES, LANES)],
                    nat.at[f, h, pl.ds(0, used), :],
                    in_sem.at[len(loads)],
                )
            )
    for load in loads:
        load.start()

    barrier = pltpu.get_barrier_semaphore()
    greeted = [(1, 0), (-1, 0)] + list(CORNERS) + [(0, d) for d in range(1, n_py)]
    for dx, dy in greeted:
        pl.semaphore_signal(barrier, inc=1, device_id=device(dx, dy), device_id_type=MESH)

    def fill(level, carry):
        at = pl.ds(level, 1)
        for k in range(3):
            consts[k, at, :] = jnp.full((1, LANES), damping[k, level], jnp.float32)
        consts[3, at, :] = jnp.full((1, LANES), exner[level], jnp.float32)
        consts[4, at, :] = jnp.full((1, LANES), sat_scale[level], jnp.float32)
        consts[5, at, :] = jnp.full((1, LANES), layer_mass[level], jnp.float32)
        return carry

    for k in range(6):
        start = levels // SUB * SUB
        consts[k, pl.ds(start, pad - start), :] = jnp.full(
            (pad - start, LANES), 1.0 if k == 3 else 0.0, jnp.float32
        )
    lax.fori_loop(0, levels, fill, 0)
    consts[6] = LATENT / consts[3]
    for f in range(4):
        for h in range(halves):
            nat[f, h, pl.ds(used, (pad - levels) * rows), :] = jnp.zeros(
                ((pad - levels) * rows, LANES), jnp.float32
            )

    loads[0].wait()
    high_count = high.shape[0]

    def upper(i, carry):
        place = spans[pl.ds(i, 1), :] // LANES
        rank = lax.broadcasted_iota(jnp.int32, (high_count, cols), 0)
        hit = jnp.where(rank == place, 1.0, 0.0).astype(jnp.bfloat16)
        high[:, pl.ds(pl.multiple_of(i * cols, cols), cols)] = hit
        return carry

    lax.fori_loop(0, rows, upper, 0)

    for load in loads[1 : 3 + 3 * halves]:
        load.wait()

    def turned(f, q, h):
        block_rows = nat[f, h, pl.ds(pl.multiple_of(q * (SUB * rows), SUB * rows), SUB * rows), :]
        return jnp.swapaxes(block_rows.reshape(SUB, rows, LANES), 0, 1)

    def turn(q, carry):
        for f in range(3):
            for h in range(halves):
                at = pl.ds(pl.multiple_of(f * pad + q * SUB, SUB), SUB)
                grid[pl.ds(2, rows), at, pl.ds(h * LANES, LANES)] = turned(f, q, h)
        return carry

    lax.fori_loop(0, pad // SUB, turn, 0)

    def turn_geometry(i, carry):
        for k in range(3):
            grid[i + 2, pl.ds(levels + k, 1), pl.ds(0, cols)] = weights[k, pl.ds(i, 1), :]
        grid[i + 2, pl.ds(levels + 3, 1), pl.ds(0, cols)] = areas[pl.ds(i, 1), :]
        return carry

    lax.fori_loop(0, rows, turn_geometry, 0)
    pl.semaphore_wait(barrier, len(greeted))

    sends = []

    def send(source, target, to):
        k = len(sends)
        copy = pltpu.make_async_remote_copy(
            src_ref=source,
            dst_ref=target,
            send_sem=send_sem.at[k],
            recv_sem=recv_sem.at[k],
            device_id=to,
            device_id_type=MESH,
        )
        copy.start()
        sends.append(copy)

    def send_rows(first, count):
        part = pl.ds(first, count)
        lanes = pl.ds(0, cols)
        send(grid.at[pl.ds(rows, 2), part, lanes], grid.at[pl.ds(0, 2), part, lanes], device(1, 0))
        send(
            grid.at[pl.ds(2, 2), part, lanes],
            grid.at[pl.ds(rows + 2, 2), part, lanes],
            device(-1, 0),
        )

    send_rows(0, 2 * pad)

    lane = lax.broadcasted_iota(jnp.int32, (SUB, LANES), 1)
    per = LANES // (2 * rows)

    def edge_tile(r, g, dy):
        first = cols - LANES if dy > 0 else 0
        at = g * SUB if isinstance(g, int) else pl.multiple_of(g * SUB, SUB)
        return grid[r, pl.ds(at, SUB), pl.ds(first, LANES)]

    def pack(q, carry):
        for side, dy in enumerate((1, -1)):
            packed = jnp.zeros((SUB, LANES), jnp.float32)
            for part in range(per):
                for i in range(rows):
                    p = (part * rows + i) * 2
                    shift = (p - (LANES - 2 if dy > 0 else 0)) % LANES
                    moved = edge_tile(i + 2, q * per + part, dy)
                    if shift:
                        moved = pltpu.roll(moved, shift, 1)
                    packed = jnp.where(lane // 2 == p // 2, moved, packed)
            col_send[side, pl.ds(pl.multiple_of(q * SUB, SUB), SUB), :] = packed
        return carry

    lax.fori_loop(0, groups // per, pack, 0)
    send(col_send.at[0], col_recv.at[0], device(0, 1))
    send(col_send.at[1], col_recv.at[1], device(0, -1))

    pair = lane // 2
    for n, (dx, dy) in enumerate(CORNERS):
        packed = jnp.zeros((SUB, LANES), jnp.float32)
        for g in range(groups):
            for k in range(2):
                p = 4 * g + 2 * k
                moved = edge_tile((rows if dx > 0 else 2) + k, g, dy)
                shift = (p + (2 if dy > 0 else 0)) % LANES
                if shift:
                    moved = pltpu.roll(moved, shift, 1)
                packed = jnp.where(pair == p // 2, moved, packed)
        corner_send[n] = packed
        send(corner_send.at[n], corner_recv.at[n], device(dx, dy))
    send_rows(2 * pad, pad)

    sends[2].wait_recv()
    sends[3].wait_recv()

    def unpack(q, carry):
        at = pl.ds(pl.multiple_of(q * SUB, SUB), SUB)
        from_left = col_recv[0, at, :]
        from_right = col_recv[1, at, :]
        for part in range(per):
            for i in range(rows):
                p = (part * rows + i) * 2
                left = pltpu.roll(from_left, (LANES - 2 - p) % LANES, 1) if p != LANES - 2 else from_left
                right = pltpu.roll(from_right, (LANES - p) % LANES, 1) if p else from_right
                g = q * per + part
                grid[i + 2, pl.ds(pl.multiple_of(g * SUB, SUB), SUB), pl.ds(cols, LANES)] = jnp.where(
                    lane < 64, right, left
                )
        return carry

    lax.fori_loop(0, groups // per, unpack, 0)

    def laplace_at(source, r, at, c):
        up = source[r + 1, at, :]
        mid = source[r, at, :]
        down = source[r - 1, at, :]
        from_right = c[3] * mid + c[4] * down
        from_left = c[5] * mid + c[6] * up
        return (
            (c[0] * up + c[1] * down)
            + c[2] * mid
            + pltpu.roll(from_right, wide - 1, 1)
            + pltpu.roll(from_left, 1, 1)
        )

    def geometry(r, k):
        return jnp.broadcast_to(grid[r, pl.ds(levels + k, 1), :], (SUB, wide))

    def first_laplace(r):
        area = geometry(r, 3)
        area_right = pltpu.roll(area, wide - 1, 1)
        ahead = area * geometry(r, 0)
        behind = area * geometry(r - 1, 0)
        to_right = area * geometry(r, 1)
        to_right_behind = area * geometry(r, 2)
        own = geometry(r, 1)
        ahead_own = geometry(r + 1, 2)
        to_left = area_right * own
        to_left_ahead = area_right * ahead_own
        centre = -(
            ahead
            + behind
            + to_right
            + to_right_behind
            + pltpu.roll(to_left, 1, 1)
            + pltpu.roll(to_left_ahead, 1, 1)
        )
        c = (
            ahead,
            behind,
            centre,
            pltpu.roll(to_right, 1, 1),
            pltpu.roll(to_right_behind, 1, 1),
            to_left,
            to_left_ahead,
        )
        for k in range(7):
            coef[r, k] = c[k]

        for g in range(2 * pad // SUB):
            at = pl.ds(g * SUB, SUB)
            lap[r, at, :] = laplace_at(grid, r, at, c)

    def coefficients(r):
        return tuple(coef[r, k] for k in range(7))

    def spread(k, at):
        tile = consts[k, at, :]
        return jnp.concatenate([tile] * halves, axis=1)

    def damped(f, r, q, c):
        at = pl.ds(f * pad + q * SUB, SUB)
        del4 = laplace_at(lap, r, at, c)[:, :cols]
        here = pl.ds(q * SUB, SUB)
        return grid[r, at, pl.ds(0, cols)] - spread(f, here) * del4

    def put(k, r, q, value):
        made[k, r - 2, pl.ds(q * SUB, SUB), :] = value

    def physics(r):
        c = coefficients(r)

        rain = jnp.zeros((SUB, cols), jnp.float32)
        for q in range(pad // SUB):
            here = pl.ds(q * SUB, SUB)
            theta_dyn = damped(0, r, q, c)
            vapor_dyn = damped(1, r, q, c)
            cloud_now = made[2, r - 2, here, :]
            temper = theta_dyn * spread(3, here)
            scale = spread(4, here)
            condensed = jnp.zeros_like(temper)
            for repeat in range(NSAT):
                warmed = temper + LATENT * condensed if repeat else temper
                saturation = scale * jnp.exp(warmed)
                excess = vapor_dyn - condensed - saturation
                slope = 1.0 + LATENT * saturation
                inverse = pl.reciprocal(slope, approx=True)
                inverse = inverse * (2.0 - slope * inverse)
                condensed = condensed + excess * inverse
            condensed = jnp.maximum(condensed, -cloud_now)
            put(0, r, q, theta_dyn + condensed * spread(6, here))
            put(1, r, q, vapor_dyn - condensed)
            liquid = cloud_now + condensed
            rained = AUTO_RATE * jnp.maximum(liquid - QCRIT, 0.0)
            put(2, r, q, liquid - rained)
            rain = rain + spread(5, here) * rained
        rain_rows[r - 2] = rain

    rank_low = lax.broadcasted_iota(jnp.int32, (LANES, cols), 0)

    def lower(i):
        total = jnp.sum(rain_rows[i], axis=0, keepdims=True)
        place = lax.rem(spans[pl.ds(i, 1), :], LANES)
        head = total.astype(jnp.bfloat16).astype(jnp.float32)
        at = pl.ds(pl.multiple_of(i * cols, cols), cols)
        hit = rank_low == place
        for k, piece in enumerate((head, total - head)):
            low[pl.ds(k * LANES, LANES), at] = jnp.where(hit, piece, 0.0).astype(jnp.bfloat16)

    def product(first, count):
        at = pl.ds(first * cols, count * cols)
        both = lax.dot_general(
            high[:, at], low[:, at], (((1,), (1,)), ((), ())), preferred_element_type=jnp.float32
        )
        return both[:, :LANES] + both[:, LANES:]

    def loop(first, end, do):
        def step(r, carry):
            do(r)
            return carry

        lax.fori_loop(first, end, step, 0)

    def twice(do, first):
        def step(n):
            do(first + 2 * n)
            do(first + 2 * n + 1)

        return step

    loop(0, (rows - 2) // 2, twice(first_laplace, 3))
    for h in range(halves):
        loads[3 + 3 * halves + h].wait()

    def turn_cloud(q, carry):
        for h in range(halves):
            at = pl.ds(pl.multiple_of(q * SUB, SUB), SUB)
            made[2, :, at, pl.ds(h * LANES, LANES)] = turned(3, q, h)
        return carry

    lax.fori_loop(0, pad // SUB, turn_cloud, 0)
    loop(0, (rows - 4) // 2, twice(physics, 4))

    def lower_four(n):
        for k in range(4):
            lower(2 + 4 * n + k)

    loop(0, (rows - 4) // 4, lower_four)
    rain_send[...] = product(2, rows - 4)

    for k in (0, 1, 4, 5, 6, 7):
        sends[k].wait_recv()

    for dx in (1, -1):
        for g in range(groups):
            for k in range(2):
                p = 4 * g + 2 * k
                left = corner_recv[CORNERS.index((dx, 1))]
                right = corner_recv[CORNERS.index((dx, -1))]
                left = pltpu.roll(left, (LANES - 2 - p) % LANES, 1) if p != LANES - 2 else left
                right = pltpu.roll(right, LANES - p, 1) if p else right
                r = k if dx > 0 else rows + 2 + k
                grid[r, pl.ds(g * SUB, SUB), pl.ds(cols, LANES)] = jnp.where(lane < 64, right, left)
    loop(0, 4, lambda n: first_laplace(n + 1 + n // 2 * (rows - 2)))
    loop(0, 4, lambda n: physics(n + 2 + n // 2 * (rows - 4)))

    for i in (0, 1, rows - 2, rows - 1):
        lower(i)

    rain_send[...] += product(0, 2) + product(rows - 2, 2)
    rains = []
    for d in range(1, n_py):
        to = device(0, d)
        copy = pltpu.make_async_remote_copy(
            src_ref=rain_send.at[pl.ds(pl.multiple_of(to[1] * block, block), block), :],
            dst_ref=rain_recv.at[d - 1],
            send_sem=rain_send_sem.at[d - 1],
            recv_sem=rain_recv_sem.at[d - 1],
            device_id=to,
            device_id_type=MESH,
        )
        copy.start()
        rains.append(copy)

    stores = []

    def turn_back(k):
        def step(q, carry):
            for h in range(halves):
                at = pl.ds(pl.multiple_of(q * SUB, SUB), SUB)
                back = jnp.swapaxes(made[k, :, at, pl.ds(h * LANES, LANES)], 0, 1)
                to = pl.ds(pl.multiple_of(q * (SUB * rows), SUB * rows), SUB * rows)
                out[k, h, to, :] = back.reshape(SUB * rows, LANES)
            return carry

        lax.fori_loop(0, pad // SUB, step, 0)

    def store(k, target):
        turn_back(k)
        for h in range(halves):
            copy = pltpu.make_async_copy(
                out.at[k, h, pl.ds(0, used), :],
                target.at[:, pl.ds(h * LANES, LANES)],
                out_sem.at[len(stores)],
            )
            copy.start()
            stores.append(copy)

    store(0, theta_out)
    store(1, vapor_out)
    store(2, cloud_out)

    for k in (8, 9):
        sends[k].wait_recv()

    def diverge_first(n):
        for r in (1 + 2 * n, 2 + 2 * n):
            c = coefficients(r)
            for g in range(2 * pad // SUB, groups):
                at = pl.ds(g * SUB, SUB)
                lap[r, at, :] = laplace_at(grid, r, at, c)

    def diverge(n):
        for r in (2 + 2 * n, 3 + 2 * n):
            c = coefficients(r)
            for q in range(pad // SUB):
                put(3, r, q, damped(2, r, q, c))

    loop(0, rows // 2 + 1, diverge_first)
    loop(0, rows // 2, diverge)
    store(3, divergence_out)

    total = rain_send[pl.ds(pl.multiple_of(py * block, block), block), :]
    for d in range(1, n_py):
        rains[d - 1].wait_recv()
        total = total + rain_recv[d - 1]
    precip_out[...] = total
    for copy in sends:
        copy.wait_send()
    for copy in rains:
        copy.wait_send()
    for copy in stores:
        copy.wait()


def placing(*refs):
    count = len(refs) // 2
    sem = refs[-1]
    copies = []
    for k in range(count):
        half = refs[k].shape[0] // 2
        for part in range(2):
            at = pl.ds(part * half, half)
            copies.append(
                pltpu.make_async_copy(refs[k].at[at], refs[count + k].at[at], sem.at[k, part])
            )
    for copy in copies:
        copy.start()
    for copy in copies:
        copy.wait()


def on_device(
    n_px,
    n_py,
    theta,
    vapor,
    cloud,
    divergence,
    edge_weight,
    inv_area,
    damping,
    exner,
    sat_scale,
    layer_mass,
    span_of,
):
    levels, rows, cols = theta.shape
    pad = (levels + 4 + SUB - 1) // SUB * SUB
    halves = cols // LANES
    wide = cols + LANES
    block = rows * cols // LANES
    flat = jax.ShapeDtypeStruct((levels * rows, cols), jnp.float32)
    f32 = jnp.float32
    anywhere = pl.BlockSpec(memory_space=pl.ANY)
    far = pl.BlockSpec(memory_space=pltpu.HBM)
    scalars = pl.BlockSpec(memory_space=pltpu.SMEM)
    made = pl.pallas_call(
        functools.partial(kernel, (n_px, n_py, levels, rows, cols)),
        out_shape=(flat, flat, flat, flat, jax.ShapeDtypeStruct((block, LANES), f32)),
        in_specs=[far] * 7 + [scalars] * 4,
        out_specs=(anywhere,) * 4 + (pl.BlockSpec(memory_space=pltpu.VMEM),),
        scratch_shapes=[
            pltpu.VMEM((4, halves, pad * rows, LANES), f32),
            pltpu.VMEM((4, halves, pad * rows, LANES), f32),
            pltpu.VMEM((4, rows, pad, cols), f32),
            pltpu.VMEM((rows + 4, 3 * pad, wide), f32),
            pltpu.VMEM((rows + 4, 3 * pad, wide), f32),
            pltpu.VMEM((rows + 4, 7, SUB, wide), f32),
            pltpu.VMEM((7, pad, LANES), f32),
            pltpu.VMEM((3, rows, cols), f32),
            pltpu.VMEM((rows, cols), f32),
            pltpu.VMEM((rows, cols), jnp.int32),
            pltpu.VMEM((2, 3 * pad * 2 * rows // LANES, LANES), f32),
            pltpu.VMEM((2, 3 * pad * 2 * rows // LANES, LANES), f32),
            pltpu.VMEM((4, SUB, LANES), f32),
            pltpu.VMEM((4, SUB, LANES), f32),
            pltpu.VMEM((n_py * block, rows * cols), jnp.bfloat16),
            pltpu.VMEM((2 * LANES, rows * cols), jnp.bfloat16),
            pltpu.VMEM((rows, SUB, cols), f32),
            pltpu.VMEM((n_py * block, LANES), f32),
            pltpu.VMEM((n_py - 1, block, LANES), f32),
            pltpu.SemaphoreType.DMA((4 * halves + 3,)),
            pltpu.SemaphoreType.DMA((4 * halves,)),
            pltpu.SemaphoreType.DMA((10,)),
            pltpu.SemaphoreType.DMA((10,)),
            pltpu.SemaphoreType.DMA((n_py - 1,)),
            pltpu.SemaphoreType.DMA((n_py - 1,)),
        ],
        compiler_params=pltpu.CompilerParams(
            collective_id=0, has_side_effects=True, vmem_limit_bytes=40 * 1024 * 1024
        ),
        cost_estimate=pl.CostEstimate(
            flops=60 * levels * rows * cols, bytes_accessed=32 * levels * rows * cols, transcendentals=0
        ),
    )(
        *[
            pltpu.with_memory_space_constraint(array, pltpu.HBM)
            for array in (
                theta.reshape(levels * rows, cols),
                vapor.reshape(levels * rows, cols),
                divergence.reshape(levels * rows, cols),
                cloud.reshape(levels * rows, cols),
                edge_weight,
                inv_area,
                span_of,
            )
        ],
        damping,
        exner,
        sat_scale,
        layer_mass,
    )
    shape = (levels, rows, cols)
    theta_next, vapor_next, cloud_next, divergence_next, precip = pl.pallas_call(
        placing,
        out_shape=tuple(jax.ShapeDtypeStruct(array.shape, array.dtype) for array in made),
        in_specs=[pl.BlockSpec(memory_space=pltpu.VMEM)] * 5,
        out_specs=(far,) * 5,
        scratch_shapes=[pltpu.SemaphoreType.DMA((len(made), 2))],
        compiler_params=pltpu.CompilerParams(vmem_limit_bytes=1024 * 1024),
    )(*[pltpu.with_memory_space_constraint(array, pltpu.VMEM) for array in made])
    return (
        theta_next.reshape(shape),
        vapor_next.reshape(shape),
        cloud_next.reshape(shape),
        divergence_next.reshape(shape),
        precip.reshape(1, block * LANES),
    )


def solution(mesh):
    placed = (
        P(None, "px", "py"),
        P(None, "px", "py"),
        P(None, "px", "py"),
        P(None, "px", "py"),
        P(None, "px", "py"),
        P("px", "py"),
        P(),
        P(),
        P(),
        P(),
        P("px", "py"),
    )
    return jax.shard_map(
        functools.partial(on_device, mesh.shape["px"], mesh.shape["py"]),
        mesh=mesh,
        in_specs=placed,
        out_specs=(
            P(None, "px", "py"),
            P(None, "px", "py"),
            P(None, "px", "py"),
            P(None, "px", "py"),
            P("px", "py"),
        ),
        check_vma=False,
    )
```
